512 devices in a mesh: ctx: 32 (over z_lo, y), tp: 8 (over z_hi, x), dp: 2 (over core).
Axes of the slice: x: 4, y: 4, z: 16 (z_hi: 2, z_lo: 8; z = z_hi * 8 + z_lo), core: 2. Of those that a mesh axis runs over, the one named last changes fastest.
Arguments:
- vis_qkv: bfloat16 [32768, 3, 1280], P(('dp', 'ctx'), None, 'tp'), parts along dimension 0, may hold values from -60 to 60
- vis_resid: bfloat16 [32768, 1280], P(('dp', 'ctx'), 'tp'), parts along dimension 0, may hold values from -1.796875 to 1.796875
- vis_out_w: bfloat16 [1280, 1280], P(None, 'tp'), may hold values from -0.15625 to 0.15625
- merge_gain: float32 [1280], P('tp'), may hold values from 0.5 to 1.5
- merge_bias: float32 [1280], P('tp'), may hold values from -3 to 3
- vis_kv_w: bfloat16 [4, 1280, 2048], P(None, 'tp'), may hold values from -0.078125 to 0.078125
- frame_host: int32 [64], P('dp'), parts along dimension 0, may hold values from 0 to 31, as said below
- vis_pos: int32 [64], P('dp'), parts along dimension 0, may hold values from 0 to 8064, as said below
- doc_ids: int32 [16384], P('dp'), parts along dimension 0, may hold values from 0 to 3, as said below
- text_kv: bfloat16 [16384, 8, 2, 128], P(('dp', 'ctx'), 'tp'), parts along dimension 0, may hold values from -4 to 4
- queries: bfloat16 [16384, 4096], P(('dp', 'ctx'), 'tp'), parts along dimension 0, may hold values from -50 to 50
Outputs:
- attended: bfloat16 [16384, 4096], P(('dp', 'ctx'), 'tp'), parts along dimension 0
The draws below stay inside these ranges and needn't reach their ends.
There are 2 independent parts, one for each index of `dp`. The reference program is written for one: setup_inputs(seed, part) draws one part's arguments, and reference() takes and returns one part's arrays. A program takes and returns all parts, laid end to end along the dimension named above; an argument that names none is the same for every part. Nothing has to cross between parts.
Inputs may be any that keep to these rules, and one draw needn't show every extreme that they name: `vis_pos`: frame starts are multiples of 128 and increase with the frame; some block of 256 positions holds only frames. `frame_host`: each frame is encoded on the ctx device that holds its positions or on the device 32 / 2 indices away along ctx; every device encodes exactly 1 frame. `doc_ids`: never falls along the sequence.
All inputs are finite; a program needn't handle non-finite values.
Results may differ from the reference program's by a relative error of at most 0.0085.
Values may be sent and summed in bfloat16 or wider, within the bound.
A program may use at most 64 MiB of HBM per device.

```python
import math
import jax
import jax.numpy as jnp
from jax import lax

VD = 1280
VH = 16
HD = 128
H = 32
KVH = 8
FT = 128
T_DEV = 256
FP = 512
FRAMES_DEV = 1
SEQ = 8192
FRAMES = 32
PATCHES = 16384
VTOK = 4096


def layout_tables(key):
    peers = SEQ // T_DEV
    half_count = peers // 2
    slot_count = T_DEV // FT
    swing = FRAMES_DEV - jax.random.randint(jax.random.fold_in(key, 11), (half_count,), 0, (FRAMES_DEV + 1) // 2 + 1)
    chosen_pair = jax.random.randint(jax.random.fold_in(key, 12), (), 0, half_count)
    swing = jnp.where(jnp.arange(half_count) == chosen_pair, FRAMES_DEV, swing)
    sign = 2 * jax.random.randint(jax.random.fold_in(key, 14), (half_count,), 0, 2) - 1
    lower_count = FRAMES_DEV + sign * swing
    counts = jnp.concatenate([lower_count, 2 * FRAMES_DEV - lower_count])
    noise = jax.random.randint(jax.random.fold_in(key, 13), (peers, slot_count), 0, 1 << 30)
    slot_rank = jnp.argsort(jnp.argsort(noise, axis=1, stable=True), axis=1, stable=True)
    chosen = slot_rank < counts[:, None]
    within = jnp.cumsum(chosen.astype(jnp.int32), axis=1) - 1
    device_ids = jnp.arange(peers)
    pair_of = device_ids % half_count
    pair_index = jnp.where(device_ids[:, None] < half_count, within, lower_count[pair_of][:, None] + within)
    pair_noise = jax.random.randint(jax.random.fold_in(key, 15), (half_count, 2 * FRAMES_DEV), 0, 1 << 30)
    pair_rank = jnp.argsort(jnp.argsort(pair_noise, axis=1, stable=True), axis=1, stable=True)
    safe_index = jnp.clip(pair_index, 0, 2 * FRAMES_DEV - 1)
    rank_here = jnp.take_along_axis(pair_rank[pair_of], safe_index, axis=1)
    host = jnp.where(rank_here < FRAMES_DEV, pair_of[:, None], pair_of[:, None] + half_count)
    candidates = (device_ids[:, None] * T_DEV + jnp.arange(slot_count)[None, :] * FT).reshape(peers * slot_count)
    flat_chosen = chosen.reshape(peers * slot_count)
    picked = jnp.argsort(jnp.where(flat_chosen, 0, 1), stable=True)[:FRAMES]
    return (candidates[picked].astype(jnp.int32), host.reshape(peers * slot_count)[picked].astype(jnp.int32))


def draw_vis_pos(key, part):
    return layout_tables(key)[0]


def draw_frame_host(key, part):
    return layout_tables(key)[1]


def doc_table(key):
    bounds = jax.random.randint(jax.random.fold_in(key, 31), (3,), 1, SEQ)
    position = jnp.arange(SEQ, dtype=jnp.int32)
    return jnp.sum(jnp.where(position[:, None] >= bounds[None, :], 1, 0), axis=1).astype(jnp.int32)


def draw_doc_ids(key, part):
    return doc_table(key)


def draw_vis_qkv(key, part):
    array_shape = (PATCHES, 3, VD)
    query_factor = jnp.where(jnp.arange(3)[None, :, None] == 0, 2.5, 1.0)
    drawn = jnp.clip(jax.random.normal(key, array_shape, jnp.float32), -4.0, 4.0) * query_factor
    return drawn.astype(jnp.bfloat16)


def language_fields(key):
    group = H // KVH
    kv_key = jax.random.fold_in(key, 21)
    query_key = jax.random.fold_in(key, 22)
    kv_all = jnp.clip(jax.random.normal(kv_key, (SEQ, KVH, 2, HD), jnp.float32), -4.0, 4.0)
    query_all = jnp.clip(2.0 * jax.random.normal(query_key, (SEQ, KVH, group, HD), jnp.float32), -8.0, 8.0)
    return (kv_all.astype(jnp.bfloat16), query_all.reshape(SEQ, H * HD).astype(jnp.bfloat16))


def draw_text_kv(key, part):
    return language_fields(key)[0]


def draw_queries(key, part):
    return language_fields(key)[1]


def block_scale(rng, dims, cuts, smallest, top_value):
    def one(dim, shards_of):
        heights = jax.random.uniform(jax.random.fold_in(jax.random.fold_in(rng, 6), dim), (shards_of,), jnp.float32, smallest / len(cuts), top_value / len(cuts))
        return jnp.repeat(jnp.exp(heights), dims[dim] // shards_of).reshape((-1,) + (1,) * (len(dims) - dim - 1))

    loudness = one(*cuts[0])
    for cut in cuts[1:]:
        loudness = loudness * one(*cut)
    return loudness


def scatter_about(rng, extent, scale, most, split=(), held_as=jnp.bfloat16):
    values = jax.random.normal(rng, extent, jnp.float32) * scale
    if len(split) > 0:
        values = block_scale(rng, extent, split, -0.22, 0.18) * values
    return jnp.clip(values, min=-most, max=most).astype(held_as)


def setup_inputs(seed: int = 0, part: int = 0) -> dict:
    seeds = jax.random.split(jax.random.key(seed), 12)
    part_splits = jax.random.split(jax.random.fold_in(seeds[11], part), 12)
    return {
        "vis_qkv": draw_vis_qkv(jax.random.fold_in(jax.random.fold_in(seeds[11], part), 71), part),
        "vis_resid": scatter_about(part_splits[1], (PATCHES, VD), 0.3, 1.796875, ((0, 32), (1, 8))),
        "vis_out_w": scatter_about(seeds[2], (VD, VD), VD ** -0.5, 0.15625, ((1, 8),)),
        "merge_gain": jnp.clip(0.5 + 1.0 * jax.random.uniform(seeds[3], (VD,), jnp.float32) ** block_scale(seeds[3], (VD,), ((0, 8),), -0.2, 0.2), 0.5, 1.5),
        "merge_bias": scatter_about(seeds[4], (VD,), 0.5, 3.0, ((0, 8),), jnp.float32),
        "vis_kv_w": scatter_about(seeds[5], (4, VD, KVH * 2 * HD), (4 * VD) ** -0.5, 0.078125, ((1, 8),)),
        "frame_host": draw_frame_host(jax.random.fold_in(jax.random.fold_in(seeds[11], part), 71), part),
        "vis_pos": draw_vis_pos(jax.random.fold_in(jax.random.fold_in(seeds[11], part), 71), part),
        "doc_ids": draw_doc_ids(jax.random.fold_in(jax.random.fold_in(seeds[11], part), 71), part),
        "text_kv": draw_text_kv(jax.random.fold_in(jax.random.fold_in(seeds[11], part), 71), part),
        "queries": draw_queries(jax.random.fold_in(jax.random.fold_in(seeds[11], part), 71), part),
    }


def frame_attention(frame_fields):
    head_dim = VD // VH
    fields = frame_fields.astype(jnp.float32)
    scores = jnp.einsum('qhd,khd->hqk', fields[:, 0], fields[:, 1]) / math.sqrt(head_dim)
    row_max = lax.optimization_barrier(jnp.max(scores, axis=2, keepdims=True))
    exponent = jnp.exp(scores - row_max)
    denominator = lax.optimization_barrier(jnp.sum(exponent, axis=2, keepdims=True))
    weights = lax.optimization_barrier(exponent.astype(jnp.bfloat16))
    mixed = jnp.einsum('hqk,khd->qhd', weights.astype(jnp.float32), fields[:, 2])
    return (mixed / jnp.transpose(denominator, (1, 0, 2))).astype(jnp.bfloat16)

def vision_part(vis_qkv, vis_resid, vis_out_w, merge_gain, merge_bias, vis_kv_w):
    head_dim = VD // VH
    framed = vis_qkv.reshape(FRAMES, FP, 3, VH, head_dim)
    context = lax.map(frame_attention, framed).reshape(PATCHES, VD)
    hidden = vis_resid.astype(jnp.float32) + jnp.dot(context, vis_out_w, preferred_element_type=jnp.float32)
    mean_value = lax.optimization_barrier(jnp.mean(hidden, axis=1, keepdims=True))
    variance = lax.optimization_barrier(jnp.mean(jnp.square(hidden - mean_value), axis=1, keepdims=True))
    normed = ((hidden - mean_value) * lax.rsqrt(variance + 1e-06) * merge_gain + merge_bias).astype(jnp.bfloat16)
    merged = normed.reshape(VTOK, 4 * VD)
    weight_flat = vis_kv_w.reshape(4 * VD, KVH * 2 * HD)
    return jnp.dot(merged, weight_flat, preferred_element_type=jnp.float32).astype(jnp.bfloat16)

def language_block(query_block, kv_prefix, allowed):

    def one_head(packed):
        query_head, key_head, value_head = packed
        scores = jnp.einsum('tgd,sd->tgs', query_head.astype(jnp.float32), key_head.astype(jnp.float32)) / math.sqrt(HD)
        scores = jnp.where(allowed[:, None, :], scores, -jnp.inf)
        row_max = lax.optimization_barrier(jnp.max(scores, axis=2, keepdims=True))
        exponent = jnp.exp(scores - row_max)
        denominator = lax.optimization_barrier(jnp.sum(exponent, axis=2, keepdims=True))
        weights = lax.optimization_barrier(exponent.astype(jnp.bfloat16))
        mixed = jnp.einsum('tgs,sd->tgd', weights.astype(jnp.float32), value_head.astype(jnp.float32))
        return (mixed / denominator).astype(jnp.bfloat16)
    heads_out = lax.map(one_head, (jnp.transpose(query_block, (1, 0, 2, 3)), jnp.transpose(kv_prefix[:, :, 0], (1, 0, 2)), jnp.transpose(kv_prefix[:, :, 1], (1, 0, 2))))
    return jnp.transpose(heads_out, (1, 0, 2, 3)).reshape(query_block.shape[0], H * HD)

def reference(vis_qkv, vis_resid, vis_out_w, merge_gain, merge_bias, vis_kv_w, frame_host, vis_pos, doc_ids, text_kv, queries):
    vision_kv = vision_part(vis_qkv, vis_resid, vis_out_w, merge_gain, merge_bias, vis_kv_w)
    frame_index = jnp.arange(FRAMES, dtype=jnp.int32)
    same_host = frame_host[:, None] == frame_host[None, :]
    earlier = frame_index[None, :] < frame_index[:, None]
    host_rank = lax.optimization_barrier(jnp.sum(jnp.where(same_host & earlier, 1, 0), axis=1)).astype(jnp.int32)
    layout_row = (frame_host * FRAMES_DEV + host_rank).astype(jnp.int32)
    by_frame = vision_kv.reshape(FRAMES, FT, KVH * 2 * HD)[layout_row]
    places = (vis_pos[:, None] + jnp.arange(FT, dtype=jnp.int32)[None, :]).reshape(VTOK).astype(jnp.int32)
    keys_values = text_kv.reshape(SEQ, KVH * 2 * HD).at[places].set(by_frame.reshape(VTOK, KVH * 2 * HD))
    keys_values = keys_values.reshape(SEQ, KVH, 2, HD)
    group = H // KVH
    query_all = queries.reshape(SEQ, KVH, group, HD)
    block_rows = math.gcd(SEQ, 512)
    position = jnp.arange(SEQ, dtype=jnp.int32)
    pieces = []
    for block_index in range(SEQ // block_rows):
        lower = block_index * block_rows
        upper = lower + block_rows
        allowed = (position[:upper][None, :] <= position[lower:upper][:, None]) & (doc_ids[:upper][None, :] == doc_ids[lower:upper][:, None])
        pieces.append(language_block(query_all[lower:upper], keys_values[:upper], allowed))
    return jnp.concatenate(pieces, axis=0)
```

```python
import functools
import math

import jax
import jax.numpy as jnp
from jax import lax
from jax.experimental import pallas as pl
from jax.experimental.pallas import tpu as pltpu
from jax.sharding import PartitionSpec as P

VD = 1280
VH = 16
HD = 128
FT = 128
FP = 512
T = 256
GROUP = 4
LOCAL = 160
HEAD = 80
CTX = 32
TP = 8
NEGATIVE = -1e30
LOG2E = math.log2(math.e)
MESH = pl.DeviceIdType.MESH
F32 = jnp.float32
BF16 = jnp.bfloat16


def dot_nt(a, b):
    return lax.dot_general(a, b, (((1,), (1,)), ((), ())), preferred_element_type=F32)


def dot_nn(a, b):
    return lax.dot_general(a, b, (((1,), (0,)), ((), ())), preferred_element_type=F32)


def eye(rows, cols, dtype):
    r = lax.broadcasted_iota(jnp.int32, (rows, cols), 0)
    c = lax.broadcasted_iota(jnp.int32, (rows, cols), 1)
    return jnp.where(r == c, 1.0, 0.0).astype(dtype)


class Gather:
    def __init__(self, buf, send_z, send_f, send_y, recv, place):
        self.buf, self.send_z, self.send_f, self.send_y, self.recv = buf, send_z, send_f, send_y, recv
        self.zl, self.y, self.tp, self.dp = place
        self.me = self.zl * 4 + self.y
        self.quad = (self.zl // 4) * 4
        self.far = lax.rem(self.zl + 4, 8)
        self.far_quad = 4 - self.quad
        self.sent = []

    def copy(self, block, sem, zl, y):
        return pltpu.make_async_remote_copy(
            src_ref=self.buf.at[block],
            dst_ref=self.buf.at[block],
            send_sem=sem,
            recv_sem=self.recv.at[block],
            device_id=(zl * 4 + y, self.tp, self.dp),
            device_id_type=MESH,
        )

    def wait_block(self, block):
        self.copy(block, self.send_z.at[0], self.far, self.y).wait_recv()

    def near(self, d):
        return self.quad + lax.rem(self.zl + d, 4)

    def start(self, copy):
        copy.start()
        self.sent.append(copy)

    def spread_y(self, slot, block):
        for d in (1, 3, 2):
            self.start(self.copy(block, self.send_y.at[slot * 3 + d - 1], self.zl, lax.rem(self.y + d, 4)))

    def first(self):
        self.start(self.copy(self.me, self.send_z.at[0], self.far, self.y))
        for d in (1, 2, 3):
            self.start(self.copy(self.me, self.send_z.at[d], self.near(d), self.y))
        self.spread_y(0, self.me)

    def take_near(self):
        for d in (1, 2, 3):
            block = self.near(d) * 4 + self.y
            self.wait_block(block)
            self.spread_y(d, block)

    def take_far(self):
        block = self.far * 4 + self.y
        self.wait_block(block)
        for d in (1, 2, 3):
            self.start(self.copy(block, self.send_f.at[d - 1], self.near(d), self.y))
        self.spread_y(4, block)

    def take_rest(self):
        for d in (1, 2, 3):
            block = (self.far_quad + lax.rem(self.zl + d, 4)) * 4 + self.y
            self.wait_block(block)
            self.spread_y(4 + d, block)

    def take_y(self):
        def layer(z, carry):
            for d in (1, 2, 3):
                self.wait_block(z * 4 + lax.rem(self.y + d, 4))
            return carry

        lax.fori_loop(0, 8, layer, 0)

    def finish(self):
        for copy in self.sent:
            copy.wait_send()


def kernel(
    qkv, resid, out_w, gain, bias, kv_w_hbm, host, pos, docs, text, queries,
    out,
    kv_w, ctx, mine, stat, part_send, part_recv, part_own, pair_send, pair_recv, perm,
    tbuf, vbuf, text_pos, frame_pos, m_s, l_s, acc_s,
    load_sem, cz_s, cz_r, cx_s, cx_r, cf_s, cf_r, st_s, st_r, rx_s, rx_r, rz_s, rz_r,
    tz_s, tf_s, ty_s, t_r, vz_s, vf_s, vy_s, v_r,
):
    c = lax.axis_index("ctx")
    tp = lax.axis_index("tp")
    dp = lax.axis_index("dp")
    zl, y = c // 4, lax.rem(c, 4)
    zh, x = tp // 4, lax.rem(tp, 4)
    other = 1 - zh

    def at_tp(h, col):
        return (c, h * 4 + col, dp)

    def x_of(d):
        return lax.rem(x + d, 4)

    barrier = pltpu.get_barrier_semaphore()
    for d in range(1, TP):
        pl.semaphore_signal(barrier, inc=1, device_id=(c, lax.rem(tp + d, TP), dp), device_id_type=MESH)
    for d in range(1, 8):
        pl.semaphore_signal(barrier, inc=1, device_id=(lax.rem(zl + d, 8) * 4 + y, tp, dp), device_id_type=MESH)
    for d in range(1, 4):
        pl.semaphore_signal(barrier, inc=1, device_id=(zl * 4 + lax.rem(y + d, 4), tp, dp), device_id_type=MESH)

    load = pltpu.make_async_copy(kv_w_hbm, kv_w, load_sem.at[0])
    load.start()
    load_text = pltpu.make_async_copy(text, tbuf.at[c], load_sem.at[1])
    load_text.start()

    texts = Gather(tbuf, tz_s, tf_s, ty_s, t_r, (zl, y, tp, dp))
    frames = Gather(vbuf, vz_s, vf_s, vy_s, v_r, (zl, y, tp, dp))

    keys = dot_nt(eye(FP, FP, BF16), qkv[1]).astype(BF16)
    sent = []
    rows_of = lambda t, h: pl.ds(pl.multiple_of(t * LOCAL + h * HEAD, 16), HEAD)

    def ctx_copy(t, h, send, recv, target):
        return pltpu.make_async_remote_copy(
            src_ref=ctx.at[rows_of(t, h)],
            dst_ref=ctx.at[rows_of(t, h)],
            send_sem=send,
            recv_sem=recv,
            device_id=target,
            device_id_type=MESH,
        )

    def begin(copy):
        copy.start()
        sent.append(copy)

    for h in range(2):
        head = slice(h * HEAD, (h + 1) * HEAD)
        scores = dot_nn(keys[:, head], qkv[0, head, :]) * (LOG2E / math.sqrt(HEAD))
        top = jnp.max(scores, axis=0, keepdims=True)
        weights = jnp.exp2(scores - top)
        total = jnp.sum(weights, axis=0, keepdims=True)
        mixed = dot_nn(qkv[2, head, :], weights.astype(BF16)) / total
        ctx[rows_of(tp, h), :] = mixed.astype(BF16)
        if h == 0:
            pl.semaphore_wait(barrier, TP - 1 + 7 + 3)
        begin(ctx_copy(tp, h, cz_s.at[h], cz_r.at[h], at_tp(other, x)))
        for d in (1, 3, 2):
            begin(ctx_copy(tp, h, cx_s.at[h * 3 + d - 1], cx_r.at[h * 3 + d - 1], at_tp(zh, x_of(d))))

    load_text.wait()
    texts.first()

    slot = lax.broadcasted_iota(jnp.int32, (64, 32), 0) * FT
    held = jnp.max(jnp.where(slot == pos[...], 1, 0), axis=1, keepdims=True)
    slot_col = lax.broadcasted_iota(jnp.int32, (64, 1), 0) * FT
    text_pos[...] = jnp.broadcast_to(jnp.where(held > 0, -1 << 20, slot_col), (64, 128))
    owner = lax.broadcasted_iota(jnp.int32, (CTX, 32), 0)
    frame_col = jnp.sum(jnp.where(owner == host[...], pos[...], 0), axis=1, keepdims=True)
    frame_pos[...] = jnp.broadcast_to(frame_col, (CTX, 128))
    doc = jnp.concatenate([docs[pl.ds(2 * c, 1), :], docs[pl.ds(2 * c + 1, 1), :]], axis=1)
    first = jnp.zeros((1, T), jnp.int32)
    for d in (1, 2, 3):
        before = jnp.sum(jnp.where(docs[...] < d, 1, 0), axis=(0, 1), keepdims=True)
        first = jnp.where(doc == d, before, first)
    query_pos = c * T + lax.broadcasted_iota(jnp.int32, (1, T), 1)
    m_s[...] = jnp.full(m_s.shape, NEGATIVE, F32)
    l_s[...] = jnp.zeros(l_s.shape, F32)
    acc_s[...] = jnp.zeros(acc_s.shape, F32)

    def attend(kv, key_pos, causal):
        k = kv[:, :HD]
        vt = kv[:, HD:].T
        allowed = key_pos >= first
        if causal:
            allowed = allowed & (key_pos <= query_pos)
        for g in range(GROUP):
            scores = dot_nt(k, queries[:, g * HD : (g + 1) * HD]) * (LOG2E / math.sqrt(HD))
            scores = jnp.where(allowed, scores, NEGATIVE)
            old = m_s[g : g + 1, :]
            new = jnp.maximum(old, jnp.max(scores, axis=0, keepdims=True))
            weights = jnp.exp2(scores - new)
            factor = jnp.exp2(old - new)
            m_s[g : g + 1, :] = new
            l_s[g : g + 1, :] = l_s[g : g + 1, :] * factor + jnp.sum(weights, axis=0, keepdims=True)
            acc_s[g] = acc_s[g] * factor + dot_nn(vt, weights.astype(BF16))

    within = lax.broadcasted_iota(jnp.int32, (FT, T), 0)

    def two(a, b):
        return jnp.concatenate([within + jnp.concatenate([a, a], axis=1), within + jnp.concatenate([b, b], axis=1)], axis=0)

    def text_block(b, causal):
        attend(tbuf[b], two(text_pos[pl.ds(2 * b, 1), :], text_pos[pl.ds(2 * b + 1, 1), :]), causal)

    def text_range(lo, hi):
        def step(b, carry):
            text_block(b, False)
            return carry

        lax.fori_loop(lo, hi, step, 0)

    r = lax.broadcasted_iota(jnp.int32, (FP, FP), 0)
    p = lax.broadcasted_iota(jnp.int32, (FP, FP), 1)
    perm[...] = jnp.where((r % FT) * 4 + r // FT == p, 1.0, 0.0).astype(BF16)
    gain_col = jnp.sum(jnp.where(eye(LOCAL, LOCAL, F32) > 0, gain[...], 0.0), axis=1, keepdims=True)
    bias_col = jnp.sum(jnp.where(eye(LOCAL, LOCAL, F32) > 0, bias[...], 0.0), axis=1, keepdims=True)

    texts.take_near()
    for h in range(2):
        ctx_copy(other * 4 + x, h, cz_s.at[h], cz_r.at[h], at_tp(other, x)).wait_recv()
        for d in (1, 3, 2):
            begin(ctx_copy(other * 4 + x, h, cf_s.at[h * 3 + d - 1], cf_r.at[h * 3 + d - 1], at_tp(zh, x_of(d))))
    texts.take_far()
    for h in range(2):
        for d in (1, 2, 3):
            ctx_copy(zh * 4 + x_of(4 - d), h, cx_s.at[0], cx_r.at[h * 3 + d - 1], at_tp(zh, x_of(d))).wait_recv()
    half = lambda i: pl.ds(pl.multiple_of(i * (VD // 2), 128), VD // 2)
    hidden = resid[...].astype(F32) + dot_nn(out_w[:, half(zh)], ctx[half(zh), :])
    for h in range(2):
        for d in (1, 2, 3):
            ctx_copy(other * 4 + x_of(4 - d), h, cf_s.at[0], cf_r.at[h * 3 + d - 1], at_tp(zh, x_of(d))).wait_recv()
    hidden = hidden + dot_nn(out_w[:, half(other)], ctx[half(other), :])
    mine[...] = hidden

    sums = jnp.sum(hidden, axis=0, keepdims=True)
    squares = jnp.sum(hidden * hidden, axis=0, keepdims=True)
    for i in range(4):
        stat[tp, i : i + 1, :] = sums[:, i * 128 : (i + 1) * 128]
        stat[tp, 4 + i : 5 + i, :] = squares[:, i * 128 : (i + 1) * 128]

    def stat_copy(t, d, target):
        return pltpu.make_async_remote_copy(
            src_ref=stat.at[t],
            dst_ref=stat.at[t],
            send_sem=st_s.at[d - 1],
            recv_sem=st_r.at[d - 1],
            device_id=(c, target, dp),
            device_id_type=MESH,
        )

    for d in range(1, TP):
        begin(stat_copy(tp, d, lax.rem(tp + d, TP)))
    texts.take_rest()
    for d in range(1, TP):
        stat_copy(lax.rem(tp + TP - d, TP), d, lax.rem(tp + d, TP)).wait_recv()
    all_stats = stat[0]
    for t in range(1, TP):
        all_stats = all_stats + stat[t]
    mean = all_stats[0:4] * (1.0 / VD)
    scale = lax.rsqrt(all_stats[4:8] * (1.0 / VD) - mean * mean + 1e-6)
    mean_row = jnp.concatenate([mean[i : i + 1] for i in range(4)], axis=1)
    scale_row = jnp.concatenate([scale[i : i + 1] for i in range(4)], axis=1)
    normed = ((mine[...] - mean_row) * scale_row * gain_col + bias_col).astype(BF16)
    grouped = dot_nt(perm[...], normed).astype(BF16)

    load.wait()

    def partial_kv(t):
        cols = pl.ds(pl.multiple_of(t * 2 * HD, 128), 2 * HD)
        total = dot_nn(grouped[:FT], kv_w[0, :, cols])
        for j in range(1, 4):
            total = total + dot_nn(grouped[j * FT : (j + 1) * FT], kv_w[j, :, cols])
        return total

    def part_copy(d):
        return pltpu.make_async_remote_copy(
            src_ref=part_send.at[d - 1],
            dst_ref=part_recv.at[d - 1],
            send_sem=rx_s.at[d - 1],
            recv_sem=rx_r.at[d - 1],
            device_id=at_tp(zh, x_of(d)),
            device_id_type=MESH,
        )

    for d in (2, 1, 3):
        for i in range(2):
            part_send[d - 1, i] = partial_kv(i * 4 + x_of(d)).astype(BF16)
        begin(part_copy(d))
    part_own[0] = partial_kv(other * 4 + x)
    part_own[1] = partial_kv(zh * 4 + x)
    for d in (1, 2, 3):
        part_copy(d).wait_recv()

    def summed(slot, which):
        total = part_own[slot]
        for d in range(3):
            total = total + part_recv[d, which].astype(F32)
        return total

    pair_send[...] = summed(0, other).astype(BF16)
    pair = pltpu.make_async_remote_copy(
        src_ref=pair_send,
        dst_ref=pair_recv,
        send_sem=rz_s.at[0],
        recv_sem=rz_r.at[0],
        device_id=at_tp(other, x),
        device_id_type=MESH,
    )
    begin(pair)
    part_own[1] = summed(1, zh)

    texts.take_y()
    middle = c // 2
    text_range(0, middle)
    pair.wait_recv()
    vbuf[c] = (part_own[1] + pair_recv[...].astype(F32)).astype(BF16)
    frames.first()
    text_range(middle, c)
    text_block(c, True)
    frames.take_near()
    frames.take_far()
    frames.take_rest()
    frames.take_y()

    def frame_step(i, carry):
        kv = jnp.concatenate([vbuf[i], vbuf[i + 16]], axis=0)
        attend(kv, two(frame_pos[pl.ds(i, 1), :], frame_pos[pl.ds(i + 16, 1), :]), True)
        return carry

    lax.fori_loop(0, jnp.minimum(c, 15) + 1, frame_step, 0)

    for g in range(GROUP):
        result = (acc_s[g] / l_s[g : g + 1, :]).astype(BF16)
        out[:, g * HD : (g + 1) * HD] = dot_nt(eye(T, T, BF16), result).astype(BF16)
    for copy in sent:
        copy.wait_send()
    texts.finish()
    frames.finish()


def shards(
    vis_qkv, vis_resid, vis_out_w, merge_gain, merge_bias, vis_kv_w, frame_host, vis_pos, doc_ids, text_kv, queries
):
    vmem = pl.BlockSpec(memory_space=pltpu.VMEM)
    hbm = pl.BlockSpec(memory_space=pl.ANY)
    dma = lambda n: pltpu.SemaphoreType.DMA((n,))
    return pl.pallas_call(
        kernel,
        out_shape=jax.ShapeDtypeStruct((T, GROUP * HD), BF16),
        in_specs=[vmem, vmem, vmem, vmem, vmem, hbm, vmem, vmem, vmem, hbm, vmem],
        out_specs=vmem,
        scratch_shapes=[
            pltpu.VMEM((4, LOCAL, 8 * 2 * HD), BF16),
            pltpu.VMEM((VD, FP), BF16),
            pltpu.VMEM((LOCAL, FP), F32),
            pltpu.VMEM((TP, 8, 128), F32),
            pltpu.VMEM((3, 2, FT, 2 * HD), BF16),
            pltpu.VMEM((3, 2, FT, 2 * HD), BF16),
            pltpu.VMEM((2, FT, 2 * HD), F32),
            pltpu.VMEM((FT, 2 * HD), BF16),
            pltpu.VMEM((FT, 2 * HD), BF16),
            pltpu.VMEM((FP, FP), BF16),
            pltpu.VMEM((CTX, T, 2 * HD), BF16),
            pltpu.VMEM((CTX, FT, 2 * HD), BF16),
            pltpu.VMEM((64, 128), jnp.int32),
            pltpu.VMEM((CTX, 128), jnp.int32),
            pltpu.VMEM((8, T), F32),
            pltpu.VMEM((8, T), F32),
            pltpu.VMEM((GROUP, HD, T), F32),
            dma(2), dma(2), dma(2), dma(6), dma(6), dma(6), dma(6), dma(7), dma(7), dma(3), dma(3), dma(1), dma(1),
            dma(4), dma(3), dma(24), dma(CTX), dma(4), dma(3), dma(24), dma(CTX),
        ],
        compiler_params=pltpu.CompilerParams(collective_id=0, has_side_effects=True, vmem_limit_bytes=48 * 2**20),
        name="window",
    )(
        jnp.transpose(vis_qkv, (1, 2, 0)),
        jnp.transpose(vis_resid),
        jnp.transpose(vis_out_w),
        merge_gain.reshape(1, LOCAL),
        merge_bias.reshape(1, LOCAL),
        vis_kv_w,
        frame_host.reshape(1, 32),
        vis_pos.reshape(1, 32),
        doc_ids.reshape(64, 128),
        text_kv.reshape(T, 2 * HD),
        queries,
    )


def solution(mesh):
    return jax.shard_map(
        shards,
        mesh=mesh,
        in_specs=(
            P(("dp", "ctx"), None, "tp"),
            P(("dp", "ctx"), "tp"),
            P(None, "tp"),
            P("tp"),
            P("tp"),
            P(None, "tp", None),
            P("dp"),
            P("dp"),
            P("dp"),
            P(("dp", "ctx"), "tp", None, None),
            P(("dp", "ctx"), "tp"),
        ),
        out_specs=P(("dp", "ctx"), "tp"),
        check_vma=False,
    )
```

```python
import functools
import math

import jax
import jax.numpy as jnp
from jax import lax
from jax.experimental import pallas as pl
from jax.experimental.pallas import tpu as pltpu
from jax.sharding import PartitionSpec as P

VD = 1280
VH = 16
HD = 128
FT = 128
FP = 512
T = 256
GROUP = 4
LOCAL = 160
HEAD = 80
CTX = 32
TP = 8
NEGATIVE = -1e30
LOG2E = math.log2(math.e)
MESH = pl.DeviceIdType.MESH
F32 = jnp.float32
BF16 = jnp.bfloat16


def dot_nt(a, b):
    return lax.dot_general(a, b, (((1,), (1,)), ((), ())), preferred_element_type=F32)


def dot_nn(a, b):
    return lax.dot_general(a, b, (((1,), (0,)), ((), ())), preferred_element_type=F32)


def eye(rows, cols, dtype):
    r = lax.broadcasted_iota(jnp.int32, (rows, cols), 0)
    c = lax.broadcasted_iota(jnp.int32, (rows, cols), 1)
    return jnp.where(r == c, 1.0, 0.0).astype(dtype)


class Spread:
    def __init__(self, buf, send, recv, place):
        self.buf, self.send, self.recv = buf, send, recv
        self.zl, self.y, self.tp, self.dp = place
        self.sent = []

    def copy(self, block, sem, zl, y):
        return pltpu.make_async_remote_copy(
            src_ref=self.buf.at[block],
            dst_ref=self.buf.at[block],
            send_sem=sem,
            recv_sem=self.recv.at[block],
            device_id=(zl * 4 + y, self.tp, self.dp),
            device_id_type=MESH,
        )

    def wait(self, block):
        self.copy(block, self.send.at[0], lax.rem(self.zl + 4, 8), self.y).wait_recv()

    def start(self, block, zl, y):
        copy = self.copy(block, self.send.at[len(self.sent)], zl, y)
        copy.start()
        self.sent.append(copy)

    def near(self, d):
        return (self.zl // 4) * 4 + lax.rem(self.zl + d, 4)

    def to_far(self, block):
        self.start(block, lax.rem(self.zl + 4, 8), self.y)

    def to_near(self, block):
        for d in (2, 1, 3):
            self.start(block, self.near(d), self.y)

    def to_y(self, block):
        for d in (2, 1, 3):
            self.start(block, self.zl, lax.rem(self.y + d, 4))

    def finish(self):
        for copy in self.sent:
            copy.wait_send()


def kernel(
    qkv_hbm, resid_hbm, out_w_hbm, gain_hbm, bias_hbm, kv_w_hbm, host_hbm, pos_hbm, docs_hbm, text, queries_hbm,
    out,
    qkv, resid, out_w, gain, bias, kv_w, host, pos, docs, queries, ctx, mine, stat, part_send, part_recv, part_own, pair_send, pair_recv, perm,
    raw, tbuf, vbuf, text_pos, frame_pos, qt, m_s, l_s, acc_s,
    load_sem, cz_s, cz_r, cx_s, cx_r, cf_s, cf_r, st_s, st_r, rx_s, rx_r, rz_s, rz_r,
    raw_s, raw_r, t_s, t_r, v_s, v_r,
):
    c = lax.axis_index("ctx")
    tp = lax.axis_index("tp")
    dp = lax.axis_index("dp")
    zl, y = c // 4, lax.rem(c, 4)
    zh, x = tp // 4, lax.rem(tp, 4)
    other = 1 - zh

    def at_tp(h, col):
        return (c, h * 4 + col, dp)

    def x_of(d):
        return lax.rem(x + d, 4)

    barrier = pltpu.get_barrier_semaphore()
    for d in range(1, TP):
        pl.semaphore_signal(barrier, inc=1, device_id=(c, lax.rem(tp + d, TP), dp), device_id_type=MESH)
    for d in range(1, 8):
        pl.semaphore_signal(barrier, inc=1, device_id=(lax.rem(zl + d, 8) * 4 + y, tp, dp), device_id_type=MESH)
    for d in range(1, 4):
        pl.semaphore_signal(barrier, inc=1, device_id=(zl * 4 + lax.rem(y + d, 4), tp, dp), device_id_type=MESH)

    loads = []
    for source, target in (
        (qkv_hbm, qkv), (text, raw.at[zl // 4]), (pos_hbm, pos), (host_hbm, host), (docs_hbm, docs), (gain_hbm, gain),
        (bias_hbm, bias), (out_w_hbm, out_w), (resid_hbm, resid), (queries_hbm, queries), (kv_w_hbm, kv_w),
    ):
        loads.append(pltpu.make_async_copy(source, target, load_sem.at[len(loads)]))
        loads[-1].start()
    load_qkv, load_text, *load_rest, load_kv_w = loads

    place = (zl, y, tp, dp)
    texts = Spread(tbuf, t_s, t_r, place)
    frames = Spread(vbuf, v_s, v_r, place)
    pair = lax.rem(c, 16)
    quarter = lax.rem(zl, 4)
    load_qkv.wait()

    keys = dot_nt(eye(FP, FP, BF16), qkv[1]).astype(BF16)
    sent = []
    rows_of = lambda t, h: pl.ds(pl.multiple_of(t * LOCAL + h * HEAD, 16), HEAD)

    def ctx_copy(t, h, send, recv, target):
        return pltpu.make_async_remote_copy(
            src_ref=ctx.at[rows_of(t, h)],
            dst_ref=ctx.at[rows_of(t, h)],
            send_sem=send,
            recv_sem=recv,
            device_id=target,
            device_id_type=MESH,
        )

    def begin(copy):
        copy.start()
        sent.append(copy)

    for h in range(2):
        head = slice(h * HEAD, (h + 1) * HEAD)
        scores = dot_nn(keys[:, head], qkv[0, head, :]) * (LOG2E / math.sqrt(HEAD))
        top = jnp.max(scores, axis=0, keepdims=True)
        weights = jnp.exp2(scores - top)
        total = jnp.sum(weights, axis=0, keepdims=True)
        mixed = dot_nn(qkv[2, head, :], weights.astype(BF16)) / total
        ctx[rows_of(tp, h), :] = mixed.astype(BF16)
        if h == 0:
            pl.semaphore_wait(barrier, TP - 1 + 7 + 3)
        begin(ctx_copy(tp, h, cz_s.at[h], cz_r.at[h], at_tp(other, x)))
        for d in (1, 3, 2):
            begin(ctx_copy(tp, h, cx_s.at[h * 3 + d - 1], cx_r.at[h * 3 + d - 1], at_tp(zh, x_of(d))))

    raw_copy = pltpu.make_async_remote_copy(
        src_ref=raw.at[zl // 4],
        dst_ref=raw.at[zl // 4],
        send_sem=raw_s.at[0],
        recv_sem=raw_r.at[0],
        device_id=(lax.rem(c + 16, CTX), tp, dp),
        device_id_type=MESH,
    )
    load_text.wait()
    for load in load_rest:
        load.wait()

    def slot_of(i):
        return FT * (2 * lax.broadcasted_iota(jnp.int32, (16, 32), 0) + (0, 1, 32, 33)[i])

    is_text = [jnp.max(jnp.where(slot_of(i) == pos[...], 1, 0), axis=1, keepdims=True) == 0 for i in range(4)]
    slots = [slot_of(i)[:, :1] for i in range(4)]
    early = jnp.where(is_text[0], slots[0], jnp.where(is_text[1], slots[1], slots[2]))
    late = jnp.where(is_text[3], slots[3], jnp.where(is_text[2], slots[2], slots[1]))
    text_pos[0] = jnp.broadcast_to(early, (16, 128))
    text_pos[1] = jnp.broadcast_to(late, (16, 128))
    owner = lax.broadcasted_iota(jnp.int32, (CTX, 32), 0)
    frame_col = jnp.sum(jnp.where(owner == host[...], pos[...], 0), axis=1, keepdims=True)
    frame_pos[...] = jnp.broadcast_to(frame_col, (CTX, 128))
    doc = jnp.concatenate([docs[pl.ds(2 * c, 1), :], docs[pl.ds(2 * c + 1, 1), :]], axis=1)
    first = jnp.zeros((1, T), jnp.int32)
    for d in (1, 2, 3):
        before = jnp.sum(jnp.where(docs[...] < d, 1, 0), axis=(0, 1), keepdims=True)
        first = jnp.where(doc == d, before, first)
    first = jnp.concatenate([first] * GROUP, axis=1)
    query_pos = c * T + lax.rem(lax.broadcasted_iota(jnp.int32, (1, GROUP * T), 1), T)
    m_s[...] = jnp.full(m_s.shape, NEGATIVE, F32)
    l_s[...] = jnp.zeros(l_s.shape, F32)
    acc_s[...] = jnp.zeros(acc_s.shape, F32)
    for g in range(GROUP):
        qt[:, g * T : (g + 1) * T] = dot_nt(eye(HD, HD, BF16), queries[:, g * HD : (g + 1) * HD]).astype(BF16)

    def attend(blocks, starts):
        within = lax.broadcasted_iota(jnp.int32, (FT, GROUP * T), 0)
        k = jnp.concatenate([b[:, :HD] for b in blocks], axis=0)
        vt = jnp.concatenate([b[:, HD:] for b in blocks], axis=1)
        key_pos = jnp.concatenate([within + jnp.concatenate([start] * 8, axis=1) for start in starts], axis=0)
        scores = dot_nn(k, qt[...]) * (LOG2E / math.sqrt(HD))
        scores = jnp.where((key_pos >= first) & (key_pos <= query_pos), scores, NEGATIVE)
        old = m_s[...]
        new = jnp.maximum(old, jnp.max(scores, axis=0, keepdims=True))
        weights = jnp.exp2(scores - new)
        factor = jnp.exp2(old - new)
        m_s[...] = new
        l_s[...] = l_s[...] * factor + jnp.sum(weights, axis=0, keepdims=True)
        acc_s[...] = acc_s[...] * factor + dot_nn(vt, weights.astype(BF16))

    def text_step(j, carry):
        layer = lax.rem(quarter + j, 4)
        for d in (1, 2, 3):
            texts.wait(layer * 4 + lax.rem(y + d, 4))

        @pl.when(layer <= zl)
        def _():
            held = [4 * layer + i for i in range(4)]
            blocks = [tbuf[h, i * FT : (i + 1) * FT] for h in held for i in range(2)]
            attend(blocks, [text_pos[i, pl.ds(h, 1), :] for h in held for i in range(2)])

        return carry

    def frame_step(j, carry):
        layer = lax.rem(quarter + j, 4)
        for far in range(2):
            for d in (1, 2, 3):
                frames.wait((layer + 4 * far) * 4 + lax.rem(y + d, 4))

        @pl.when(layer <= zl)
        def _():
            held = [4 * layer + i + 16 * far for far in range(2) for i in range(4)]
            attend([vbuf[h] for h in held], [frame_pos[pl.ds(h, 1), :] for h in held])

        return carry

    r = lax.broadcasted_iota(jnp.int32, (FP, FP), 0)
    p = lax.broadcasted_iota(jnp.int32, (FP, FP), 1)
    perm[...] = jnp.where((r % FT) * 4 + r // FT == p, 1.0, 0.0).astype(BF16)
    gain_col = jnp.sum(jnp.where(eye(LOCAL, LOCAL, F32) > 0, gain[...], 0.0), axis=1, keepdims=True)
    bias_col = jnp.sum(jnp.where(eye(LOCAL, LOCAL, F32) > 0, bias[...], 0.0), axis=1, keepdims=True)

    for h in range(2):
        ctx_copy(other * 4 + x, h, cz_s.at[h], cz_r.at[h], at_tp(other, x)).wait_recv()
        for d in (1, 3, 2):
            begin(ctx_copy(other * 4 + x, h, cf_s.at[h * 3 + d - 1], cf_r.at[h * 3 + d - 1], at_tp(zh, x_of(d))))
    begin(raw_copy)
    for h in range(2):
        for d in (1, 2, 3):
            ctx_copy(zh * 4 + x_of(4 - d), h, cx_s.at[0], cx_r.at[h * 3 + d - 1], at_tp(zh, x_of(d))).wait_recv()
    half = lambda i: pl.ds(pl.multiple_of(i * (VD // 2), 128), VD // 2)
    hidden = resid[...].astype(F32) + dot_nn(out_w[:, half(zh)], ctx[half(zh), :])
    for h in range(2):
        for d in (1, 2, 3):
            ctx_copy(other * 4 + x_of(4 - d), h, cf_s.at[0], cf_r.at[h * 3 + d - 1], at_tp(zh, x_of(d))).wait_recv()
    hidden = hidden + dot_nn(out_w[:, half(other)], ctx[half(other), :])
    mine[...] = hidden

    sums = jnp.sum(hidden, axis=0, keepdims=True)
    squares = jnp.sum(hidden * hidden, axis=0, keepdims=True)
    for i in range(4):
        stat[tp, i : i + 1, :] = sums[:, i * 128 : (i + 1) * 128]
        stat[tp, 4 + i : 5 + i, :] = squares[:, i * 128 : (i + 1) * 128]

    def stat_copy(t, d, target):
        return pltpu.make_async_remote_copy(
            src_ref=stat.at[t],
            dst_ref=stat.at[t],
            send_sem=st_s.at[d - 1],
            recv_sem=st_r.at[d - 1],
            device_id=(c, target, dp),
            device_id_type=MESH,
        )

    for d in range(1, TP):
        begin(stat_copy(tp, d, lax.rem(tp + d, TP)))
    raw_copy.wait_recv()
    four = [raw[i, j * FT : (j + 1) * FT, :].astype(F32) for i in range(2) for j in range(2)]
    for which in range(2):
        start = text_pos[which, pl.ds(pair, 1), :]
        start = jnp.concatenate([start, start], axis=1)
        chosen = four[3]
        for i in range(3):
            chosen = jnp.where(start == FT * (2 * pair + (0, 1, 32)[i]), four[i], chosen)
        tbuf[pair, which * FT : (which + 1) * FT, :HD] = chosen[:, :HD].astype(BF16)
        tbuf[pair, which * FT : (which + 1) * FT, HD:] = chosen[:, HD:].T.astype(BF16)
    texts.to_near(pair)
    texts.to_y(pair)
    for d in range(1, TP):
        stat_copy(lax.rem(tp + TP - d, TP), d, lax.rem(tp + d, TP)).wait_recv()
    all_stats = stat[0]
    for t in range(1, TP):
        all_stats = all_stats + stat[t]
    mean = all_stats[0:4] * (1.0 / VD)
    scale = lax.rsqrt(all_stats[4:8] * (1.0 / VD) - mean * mean + 1e-6)
    mean_row = jnp.concatenate([mean[i : i + 1] for i in range(4)], axis=1)
    scale_row = jnp.concatenate([scale[i : i + 1] for i in range(4)], axis=1)
    normed = ((mine[...] - mean_row) * scale_row * gain_col + bias_col).astype(BF16)
    grouped = dot_nt(perm[...], normed).astype(BF16)

    load_kv_w.wait()

    def partial_kv(t):
        cols = pl.ds(pl.multiple_of(t * 2 * HD, 128), 2 * HD)
        total = dot_nn(grouped[:FT], kv_w[0, :, cols])
        for j in range(1, 4):
            total = total + dot_nn(grouped[j * FT : (j + 1) * FT], kv_w[j, :, cols])
        return total

    def part_copy(d):
        return pltpu.make_async_remote_copy(
            src_ref=part_send.at[d - 1],
            dst_ref=part_recv.at[d - 1],
            send_sem=rx_s.at[d - 1],
            recv_sem=rx_r.at[d - 1],
            device_id=at_tp(zh, x_of(d)),
            device_id_type=MESH,
        )

    for d in (2, 1, 3):
        for i in range(2):
            part_send[d - 1, i] = partial_kv(i * 4 + x_of(d)).astype(BF16)
        begin(part_copy(d))
    part_own[0] = partial_kv(other * 4 + x)
    part_own[1] = partial_kv(zh * 4 + x)
    for d in (2, 1, 3):
        block = lax.rem(quarter + d, 4) * 4 + y
        texts.wait(block)
        texts.to_y(block)
    for d in (1, 2, 3):
        part_copy(d).wait_recv()

    def summed(slot, which):
        total = part_own[slot]
        for d in range(3):
            total = total + part_recv[d, which].astype(F32)
        return total

    pair_send[...] = summed(0, other).astype(BF16)
    last = pltpu.make_async_remote_copy(
        src_ref=pair_send,
        dst_ref=pair_recv,
        send_sem=rz_s.at[0],
        recv_sem=rz_r.at[0],
        device_id=at_tp(other, x),
        device_id_type=MESH,
    )
    begin(last)
    part_own[1] = summed(1, zh)
    text_step(0, 0)
    last.wait_recv()
    own_kv = part_own[1] + pair_recv[...].astype(F32)
    vbuf[c, :, :HD] = own_kv[:, :HD].astype(BF16)
    vbuf[c, :, HD:] = own_kv[:, HD:].T.astype(BF16)
    frames.to_far(c)
    frames.to_near(c)
    frames.to_y(c)
    lax.fori_loop(1, 3, text_step, 0)
    far = lax.rem(c + 16, CTX)
    frames.wait(far)
    frames.to_near(far)
    frames.to_y(far)
    for d in (2, 1, 3):
        block = frames.near(d) * 4 + y
        frames.wait(block)
        frames.to_y(block)
    for d in (2, 1, 3):
        block = lax.rem(frames.near(d) + 4, 8) * 4 + y
        frames.wait(block)
        frames.to_y(block)
    lax.fori_loop(3, 4, text_step, 0)
    lax.fori_loop(0, 4, frame_step, 0)

    for g in range(GROUP):
        cols = slice(g * T, (g + 1) * T)
        result = (acc_s[:, cols] / l_s[:, cols]).astype(BF16)
        out[:, g * HD : (g + 1) * HD] = dot_nt(eye(T, T, BF16), result).astype(BF16)
    for copy in sent:
        copy.wait_send()
    texts.finish()
    frames.finish()


def shards(
    vis_qkv, vis_resid, vis_out_w, merge_gain, merge_bias, vis_kv_w, frame_host, vis_pos, doc_ids, text_kv, queries
):
    vmem = pl.BlockSpec(memory_space=pltpu.VMEM)
    hbm = pl.BlockSpec(memory_space=pl.ANY)
    dma = lambda n: pltpu.SemaphoreType.DMA((n,))
    return pl.pallas_call(
        kernel,
        out_shape=jax.ShapeDtypeStruct((T, GROUP * HD), BF16),
        in_specs=[hbm] * 11,
        out_specs=vmem,
        scratch_shapes=[
            pltpu.VMEM((3, LOCAL, FP), BF16),
            pltpu.VMEM((LOCAL, FP), BF16),
            pltpu.VMEM((LOCAL, VD), BF16),
            pltpu.VMEM((1, LOCAL), F32),
            pltpu.VMEM((1, LOCAL), F32),
            pltpu.VMEM((4, LOCAL, 8 * 2 * HD), BF16),
            pltpu.VMEM((1, 32), jnp.int32),
            pltpu.VMEM((1, 32), jnp.int32),
            pltpu.VMEM((64, 128), jnp.int32),
            pltpu.VMEM((T, GROUP * HD), BF16),
            pltpu.VMEM((VD, FP), BF16),
            pltpu.VMEM((LOCAL, FP), F32),
            pltpu.VMEM((TP, 8, 128), F32),
            pltpu.VMEM((3, 2, FT, 2 * HD), BF16),
            pltpu.VMEM((3, 2, FT, 2 * HD), BF16),
            pltpu.VMEM((2, FT, 2 * HD), F32),
            pltpu.VMEM((FT, 2 * HD), BF16),
            pltpu.VMEM((FT, 2 * HD), BF16),
            pltpu.VMEM((FP, FP), BF16),
            pltpu.VMEM((2, T, 2 * HD), BF16),
            pltpu.VMEM((16, T, 2 * HD), BF16),
            pltpu.VMEM((CTX, FT, 2 * HD), BF16),
            pltpu.VMEM((2, 16, 128), jnp.int32),
            pltpu.VMEM((CTX, 128), jnp.int32),
            pltpu.VMEM((HD, GROUP * T), BF16),
            pltpu.VMEM((1, GROUP * T), F32),
            pltpu.VMEM((1, GROUP * T), F32),
            pltpu.VMEM((HD, GROUP * T), F32),
            dma(11), dma(2), dma(2), dma(6), dma(6), dma(6), dma(6), dma(7), dma(7), dma(3), dma(3), dma(1), dma(1),
            dma(1), dma(1), dma(15), dma(16), dma(31), dma(CTX),
        ],
        compiler_params=pltpu.CompilerParams(collective_id=0, has_side_effects=True, vmem_limit_bytes=60 * 2**20),
        name="window",
    )(
        jnp.transpose(vis_qkv, (1, 2, 0)),
        jnp.transpose(vis_resid),
        jnp.transpose(vis_out_w),
        merge_gain.reshape(1, LOCAL),
        merge_bias.reshape(1, LOCAL),
        vis_kv_w,
        frame_host.reshape(1, 32),
        vis_pos.reshape(1, 32),
        doc_ids.reshape(64, 128),
        text_kv.reshape(T, 2 * HD),
        queries,
    )


def solution(mesh):
    return jax.shard_map(
        shards,
        mesh=mesh,
        in_specs=(
            P(("dp", "ctx"), None, "tp"),
            P(("dp", "ctx"), "tp"),
            P(None, "tp"),
            P("tp"),
            P("tp"),
            P(None, "tp", None),
            P("dp"),
            P("dp"),
            P("dp"),
            P(("dp", "ctx"), "tp", None, None),
            P(("dp", "ctx"), "tp"),
        ),
        out_specs=P(("dp", "ctx"), "tp"),
        check_vma=False,
    )
```

```python
import functools
import math

import jax
import jax.numpy as jnp
from jax import lax
from jax.experimental import pallas as pl
from jax.experimental.pallas import tpu as pltpu
from jax.sharding import PartitionSpec as P

VD = 1280
VH = 16
HD = 128
FT = 128
FP = 512
T = 256
GROUP = 4
LOCAL = 160
HEAD = 80
CTX = 32
TP = 8
PARTS = 2
WIDTH = FP // PARTS
TOKENS = FT // PARTS
NEGATIVE = -1e30
LOG2E = math.log2(math.e)
MESH = pl.DeviceIdType.MESH
F32 = jnp.float32
BF16 = jnp.bfloat16


def dot_nt(a, b):
    return lax.dot_general(a, b, (((1,), (1,)), ((), ())), preferred_element_type=F32)


def dot_nn(a, b):
    return lax.dot_general(a, b, (((1,), (0,)), ((), ())), preferred_element_type=F32)


def eye(rows, cols, dtype):
    r = lax.broadcasted_iota(jnp.int32, (rows, cols), 0)
    c = lax.broadcasted_iota(jnp.int32, (rows, cols), 1)
    return jnp.where(r == c, 1.0, 0.0).astype(dtype)


class Spread:
    def __init__(self, buf, send, recv, place):
        self.buf, self.send, self.recv = buf, send, recv
        self.zl, self.y, self.tp, self.dp = place
        self.sent = []

    def copy(self, block, sem, zl, y):
        return pltpu.make_async_remote_copy(
            src_ref=self.buf.at[block],
            dst_ref=self.buf.at[block],
            send_sem=sem,
            recv_sem=self.recv.at[block],
            device_id=(zl * 4 + y, self.tp, self.dp),
            device_id_type=MESH,
        )

    def wait(self, block):
        self.copy(block, self.send.at[0], lax.rem(self.zl + 4, 8), self.y).wait_recv()

    def start(self, block, zl, y):
        copy = self.copy(block, self.send.at[len(self.sent)], zl, y)
        copy.start()
        self.sent.append(copy)

    def near(self, d):
        return (self.zl // 4) * 4 + lax.rem(self.zl + d, 4)

    def to_far(self, block):
        self.start(block, lax.rem(self.zl + 4, 8), self.y)

    def to_near(self, block):
        for d in (2, 3, 1):
            self.start(block, self.near(d), self.y)

    def to_y(self, block):
        for d in (2, 1, 3):
            self.start(block, self.zl, lax.rem(self.y + d, 4))

    def finish(self):
        for copy in self.sent:
            copy.wait_send()


def kernel(
    qkv_hbm, resid_hbm, out_w_hbm, gain_hbm, bias_hbm, kv_w_hbm, host_hbm, pos_hbm, docs_hbm, text, queries_hbm,
    out,
    qkv, resid, out_w, gain, bias, kv_w, host, pos, docs, queries, ctx, mine, stat, part_send, part_recv, part_own, pair_send, pair_recv, perm,
    raw, tbuf, vbuf, text_pos, frame_pos, qt, m_s, l_s, acc_s,
    load_sem, cz_s, cz_r, cx_s, cx_r, cf_s, cf_r, st_s, st_r, rx_s, rx_r, rz_s, rz_r,
    known, raw_s, raw_r, t_s, t_r, v_s, v_r,
):
    c = lax.axis_index("ctx")
    tp = lax.axis_index("tp")
    dp = lax.axis_index("dp")
    zl, y = c // 4, lax.rem(c, 4)
    zh, x = tp // 4, lax.rem(tp, 4)
    other = 1 - zh

    def at_tp(h, col):
        return (c, h * 4 + col, dp)

    def x_of(d):
        return lax.rem(x + d, 4)

    def along_z(d):
        z = lax.rem(zh * 8 + zl + d, 16)
        return (lax.rem(z, 8) * 4 + y, (z // 8) * 4 + x, dp)

    barrier = pltpu.get_barrier_semaphore()
    contacts = [along_z(4), along_z(12)]
    for d in (1, 2, 3):
        contacts.append(at_tp(zh, x_of(d)))
        contacts.append((zl * 4 + lax.rem(y + d, 4), tp, dp))
        contacts.append((((zl // 4) * 4 + lax.rem(zl + d, 4)) * 4 + y, tp, dp))
    for contact in contacts:
        pl.semaphore_signal(barrier, inc=1, device_id=contact, device_id_type=MESH)

    loads = []
    for source, target in (
        (qkv_hbm, qkv), (text, raw.at[zl // 4]), (pos_hbm, pos), (host_hbm, host), (docs_hbm, docs), (gain_hbm, gain),
        (bias_hbm, bias), (out_w_hbm, out_w), (resid_hbm, resid), (queries_hbm, queries), (kv_w_hbm, kv_w),
    ):
        loads.append(pltpu.make_async_copy(source, target, load_sem.at[len(loads)]))
        loads[-1].start()
    load_qkv, load_text, *load_rest, load_kv_w = loads

    place = (zl, y, tp, dp)
    texts = Spread(tbuf, t_s, t_r, place)
    frames = [Spread(vbuf.at[a], v_s.at[a], v_r.at[a], place) for a in range(PARTS)]
    pair = lax.rem(c, 16)
    quarter = lax.rem(zl, 4)
    load_qkv.wait()

    keys = dot_nt(eye(FP, FP, BF16), qkv[1]).astype(BF16)
    sent = []

    def ctx_copy(a, t, send, recv, target):
        rows = pl.ds(pl.multiple_of(t * LOCAL, 16), LOCAL)
        return pltpu.make_async_remote_copy(
            src_ref=ctx.at[a, rows],
            dst_ref=ctx.at[a, rows],
            send_sem=send,
            recv_sem=recv,
            device_id=target,
            device_id_type=MESH,
        )

    def begin(copy):
        copy.start()
        sent.append(copy)

    raw_copy = pltpu.make_async_remote_copy(
        src_ref=raw.at[zl // 4],
        dst_ref=raw.at[zl // 4],
        send_sem=raw_s.at[0],
        recv_sem=raw_r.at[0],
        device_id=(lax.rem(c + 16, CTX), tp, dp),
        device_id_type=MESH,
    )
    for h in range(2):
        head = slice(h * HEAD, (h + 1) * HEAD)
        scores = dot_nn(keys[:, head], qkv[0, head, :]) * (LOG2E / math.sqrt(HEAD))
        top = jnp.max(scores, axis=0, keepdims=True)
        weights = jnp.exp2(scores - top)
        total = jnp.sum(weights, axis=0, keepdims=True)
        mixed = (dot_nn(qkv[2, head, :], weights.astype(BF16)) / total).astype(BF16)
        for a in range(PARTS):
            ctx[a, pl.ds(pl.multiple_of(tp * LOCAL + h * HEAD, 16), HEAD), :] = mixed[:, a * WIDTH : (a + 1) * WIDTH]
        if h == 0:
            pl.semaphore_wait(barrier, len(contacts))
            for i, d in enumerate((4, 12)):
                pl.semaphore_signal(known.at[i], inc=1, device_id=along_z(d), device_id_type=MESH)
    load_text.wait()
    pl.semaphore_wait(known.at[0], 1)
    pl.semaphore_wait(known.at[1], 1)
    for a in range(PARTS):
        begin(ctx_copy(a, tp, cz_s.at[a], cz_r.at[a], at_tp(other, x)))
    for a in range(PARTS):
        for d in (2, 1, 3):
            begin(ctx_copy(a, tp, cx_s.at[a * 3 + d - 1], cx_r.at[a * 3 + d - 1], at_tp(zh, x_of(d))))

    for load in load_rest:
        load.wait()

    def slot_of(i):
        return FT * (2 * lax.broadcasted_iota(jnp.int32, (16, 32), 0) + (0, 1, 32, 33)[i])

    is_text = [jnp.max(jnp.where(slot_of(i) == pos[...], 1, 0), axis=1, keepdims=True) == 0 for i in range(4)]
    slots = [slot_of(i)[:, :1] for i in range(4)]
    early = jnp.where(is_text[0], slots[0], jnp.where(is_text[1], slots[1], slots[2]))
    late = jnp.where(is_text[3], slots[3], jnp.where(is_text[2], slots[2], slots[1]))
    text_pos[0] = jnp.broadcast_to(early, (16, 128))
    text_pos[1] = jnp.broadcast_to(late, (16, 128))
    owner = lax.broadcasted_iota(jnp.int32, (CTX, 32), 0)
    frame_col = jnp.sum(jnp.where(owner == host[...], pos[...], 0), axis=1, keepdims=True)
    frame_pos[...] = jnp.broadcast_to(frame_col, (CTX, 128))
    doc = jnp.concatenate([docs[pl.ds(2 * c, 1), :], docs[pl.ds(2 * c + 1, 1), :]], axis=1)
    first = jnp.zeros((1, T), jnp.int32)
    for d in (1, 2, 3):
        before = jnp.sum(jnp.where(docs[...] < d, 1, 0), axis=(0, 1), keepdims=True)
        first = jnp.where(doc == d, before, first)
    first = jnp.concatenate([first] * GROUP, axis=1)
    query_pos = c * T + lax.rem(lax.broadcasted_iota(jnp.int32, (1, GROUP * T), 1), T)
    m_s[...] = jnp.full(m_s.shape, NEGATIVE, F32)
    l_s[...] = jnp.zeros(l_s.shape, F32)
    acc_s[...] = jnp.zeros(acc_s.shape, F32)
    for g in range(GROUP):
        qt[:, g * T : (g + 1) * T] = dot_nt(eye(HD, HD, BF16), queries[:, g * HD : (g + 1) * HD]).astype(BF16)

    def attend(k, vt, starts):
        within = lax.broadcasted_iota(jnp.int32, (k.shape[0] // len(starts), GROUP * T), 0)
        key_pos = jnp.concatenate([within + jnp.concatenate([start] * 8, axis=1) for start in starts], axis=0)
        scores = dot_nn(k, qt[...]) * (LOG2E / math.sqrt(HD))
        scores = jnp.where((key_pos >= first) & (key_pos <= query_pos), scores, NEGATIVE)
        old = m_s[...]
        new = jnp.maximum(old, jnp.max(scores, axis=0, keepdims=True))
        weights = jnp.exp2(scores - new)
        factor = jnp.exp2(old - new)
        m_s[...] = new
        l_s[...] = l_s[...] * factor + jnp.sum(weights, axis=0, keepdims=True)
        acc_s[...] = acc_s[...] * factor + dot_nn(vt, weights.astype(BF16))

    def text_step(j, carry):
        layer = lax.rem(quarter + j, 4)
        for d in (1, 2, 3):
            texts.wait(layer * 4 + lax.rem(y + d, 4))

        @pl.when(layer <= zl)
        def _():
            held = [4 * layer + i for i in range(4)]
            blocks = [tbuf[h, i * FT : (i + 1) * FT] for h in held for i in range(2)]
            k = jnp.concatenate([b[:, :HD] for b in blocks], axis=0)
            vt = jnp.concatenate([b[:, HD:] for b in blocks], axis=1)
            attend(k, vt, [text_pos[i, pl.ds(h, 1), :] for h in held for i in range(2)])

        return carry

    def frame_step(a, j):
        layer = lax.rem(quarter + j, 4)
        for far in range(2):
            for d in (1, 2, 3):
                frames[a].wait((layer + 4 * far) * 4 + lax.rem(y + d, 4))

        @pl.when(layer <= zl)
        def _():
            held = [4 * layer + i + 16 * far for far in range(2) for i in range(4)]
            k = jnp.concatenate([vbuf[a, h, :, :HD] for h in held], axis=0)
            v = jnp.concatenate([vbuf[a, h, :, HD:] for h in held], axis=0)
            attend(k, v.T, [frame_pos[pl.ds(h, 1), :] + a * TOKENS for h in held])

    r = lax.broadcasted_iota(jnp.int32, (WIDTH, WIDTH), 0)
    p = lax.broadcasted_iota(jnp.int32, (WIDTH, WIDTH), 1)
    perm[...] = jnp.where((r % TOKENS) * 4 + r // TOKENS == p, 1.0, 0.0).astype(BF16)
    gain_col = jnp.sum(jnp.where(eye(LOCAL, LOCAL, F32) > 0, gain[...], 0.0), axis=1, keepdims=True)
    bias_col = jnp.sum(jnp.where(eye(LOCAL, LOCAL, F32) > 0, bias[...], 0.0), axis=1, keepdims=True)

    def compact():
        raw_copy.wait_recv()
        four = [raw[i, j * FT : (j + 1) * FT, :].astype(F32) for i in range(2) for j in range(2)]
        for which in range(2):
            start = text_pos[which, pl.ds(pair, 1), :]
            start = jnp.concatenate([start, start], axis=1)
            chosen = four[3]
            for i in range(3):
                chosen = jnp.where(start == FT * (2 * pair + (0, 1, 32)[i]), four[i], chosen)
            tbuf[pair, which * FT : (which + 1) * FT, :HD] = chosen[:, :HD].astype(BF16)
            tbuf[pair, which * FT : (which + 1) * FT, HD:] = chosen[:, HD:].T.astype(BF16)
        texts.to_near(pair)
        texts.to_y(pair)

    for a in range(PARTS):
        ctx_copy(a, other * 4 + x, cz_s.at[a], cz_r.at[a], at_tp(other, x)).wait_recv()
        for d in (2, 1, 3):
            begin(ctx_copy(a, other * 4 + x, cf_s.at[a * 3 + d - 1], cf_r.at[a * 3 + d - 1], at_tp(zh, x_of(d))))
        if a == 0:
            begin(raw_copy)
    half = lambda i: pl.ds(pl.multiple_of(i * (VD // 2), 128), VD // 2)

    def stat_copy(a, t, d, target):
        return pltpu.make_async_remote_copy(
            src_ref=stat.at[a, t],
            dst_ref=stat.at[a, t],
            send_sem=st_s.at[a * 7 + d - 1],
            recv_sem=st_r.at[a * 7 + d - 1],
            device_id=(c, target, dp),
            device_id_type=MESH,
        )

    lanes = WIDTH // 128
    for a in range(PARTS):
        for d in (1, 2, 3):
            ctx_copy(a, zh * 4 + x_of(4 - d), cx_s.at[0], cx_r.at[a * 3 + d - 1], at_tp(zh, x_of(d))).wait_recv()
        hidden = resid[:, a * WIDTH : (a + 1) * WIDTH].astype(F32) + dot_nn(out_w[:, half(zh)], ctx[a, half(zh), :])
        for d in (1, 2, 3):
            ctx_copy(a, other * 4 + x_of(4 - d), cf_s.at[0], cf_r.at[a * 3 + d - 1], at_tp(zh, x_of(d))).wait_recv()
        hidden = hidden + dot_nn(out_w[:, half(other)], ctx[a, half(other), :])
        mine[a] = hidden
        sums = jnp.sum(hidden, axis=0, keepdims=True)
        squares = jnp.sum(hidden * hidden, axis=0, keepdims=True)
        stat[a, tp] = jnp.zeros((8, 128), F32)
        for i in range(lanes):
            stat[a, tp, i : i + 1, :] = sums[:, i * 128 : (i + 1) * 128]
            stat[a, tp, 4 + i : 5 + i, :] = squares[:, i * 128 : (i + 1) * 128]
        for d in (6, 2, 4, 5, 3, 1, 7):
            begin(stat_copy(a, tp, d, lax.rem(tp + d, TP)))

    load_kv_w.wait()

    def part_copy(a, d):
        return pltpu.make_async_remote_copy(
            src_ref=part_send.at[a, d - 1],
            dst_ref=part_recv.at[a, d - 1],
            send_sem=rx_s.at[a * 3 + d - 1],
            recv_sem=rx_r.at[a * 3 + d - 1],
            device_id=at_tp(zh, x_of(d)),
            device_id_type=MESH,
        )

    for a in range(PARTS):
        for d in range(1, TP):
            stat_copy(a, lax.rem(tp + TP - d, TP), d, lax.rem(tp + d, TP)).wait_recv()
        all_stats = stat[a, 0]
        for t in range(1, TP):
            all_stats = all_stats + stat[a, t]
        mean = all_stats[0:4] * (1.0 / VD)
        scale = lax.rsqrt(all_stats[4:8] * (1.0 / VD) - mean * mean + 1e-6)
        mean_row = jnp.concatenate([mean[i : i + 1] for i in range(lanes)], axis=1)
        scale_row = jnp.concatenate([scale[i : i + 1] for i in range(lanes)], axis=1)
        normed = ((mine[a] - mean_row) * scale_row * gain_col + bias_col).astype(BF16)
        grouped = dot_nt(perm[...], normed).astype(BF16)

        def partial_kv(t):
            cols = pl.ds(pl.multiple_of(t * 2 * HD, 128), 2 * HD)
            total = dot_nn(grouped[:TOKENS], kv_w[0, :, cols])
            for j in range(1, 4):
                total = total + dot_nn(grouped[j * TOKENS : (j + 1) * TOKENS], kv_w[j, :, cols])
            return total

        for d in (2, 1, 3):
            for i in range(2):
                part_send[a, d - 1, i] = partial_kv(i * 4 + x_of(d)).astype(BF16)
            begin(part_copy(a, d))
        if a == 0:
            compact()
        part_own[a, 0] = partial_kv(other * 4 + x)
        part_own[a, 1] = partial_kv(zh * 4 + x)

    def summed(a, slot, which):
        total = part_own[a, slot]
        for d in range(3):
            total = total + part_recv[a, d, which].astype(F32)
        return total

    def pair_copy(a):
        return pltpu.make_async_remote_copy(
            src_ref=pair_send.at[a],
            dst_ref=pair_recv.at[a],
            send_sem=rz_s.at[a],
            recv_sem=rz_r.at[a],
            device_id=at_tp(other, x),
            device_id_type=MESH,
        )

    for a in range(PARTS):
        for d in (1, 2, 3):
            part_copy(a, d).wait_recv()
        pair_send[a] = summed(a, 0, other).astype(BF16)
        begin(pair_copy(a))
        part_own[a, 1] = summed(a, 1, zh)
    for d in (2, 1, 3):
        block = lax.rem(quarter + d, 4) * 4 + y
        texts.wait(block)
        texts.to_y(block)
    text_step(0, 0)
    far = lax.rem(c + 16, CTX)
    for a in range(PARTS):
        pair_copy(a).wait_recv()
        vbuf[a, c] = (part_own[a, 1] + pair_recv[a].astype(F32)).astype(BF16)
        frames[a].to_far(c)
        frames[a].to_near(c)
        frames[a].to_y(c)
    for a in range(PARTS):
        frames[a].wait(far)
        frames[a].to_near(far)
        frames[a].to_y(far)
        for d in (2, 1, 3):
            block = frames[a].near(d) * 4 + y
            frames[a].wait(block)
            frames[a].to_y(block)
    lax.fori_loop(1, 3, text_step, 0)
    for a in range(PARTS):
        for d in (2, 1, 3):
            block = lax.rem(frames[a].near(d) + 4, 8) * 4 + y
            frames[a].wait(block)
            frames[a].to_y(block)
    lax.fori_loop(3, 4, text_step, 0)
    for a in range(PARTS):

        def step(j, carry):
            frame_step(a, j)
            return carry

        lax.fori_loop(0, 4, step, 0)

    for g in range(GROUP):
        cols = slice(g * T, (g + 1) * T)
        result = (acc_s[:, cols] / l_s[:, cols]).astype(BF16)
        out[:, g * HD : (g + 1) * HD] = dot_nt(eye(T, T, BF16), result).astype(BF16)
    for copy in sent:
        copy.wait_send()
    texts.finish()
    for part in frames:
        part.finish()


def shards(
    vis_qkv, vis_resid, vis_out_w, merge_gain, merge_bias, vis_kv_w, frame_host, vis_pos, doc_ids, text_kv, queries
):
    vmem = pl.BlockSpec(memory_space=pltpu.VMEM)
    hbm = pl.BlockSpec(memory_space=pl.ANY)
    dma = lambda n: pltpu.SemaphoreType.DMA((n,))
    return pl.pallas_call(
        kernel,
        out_shape=jax.ShapeDtypeStruct((T, GROUP * HD), BF16),
        in_specs=[hbm] * 11,
        out_specs=vmem,
        scratch_shapes=[
            pltpu.VMEM((3, LOCAL, FP), BF16),
            pltpu.VMEM((LOCAL, FP), BF16),
            pltpu.VMEM((LOCAL, VD), BF16),
            pltpu.VMEM((1, LOCAL), F32),
            pltpu.VMEM((1, LOCAL), F32),
            pltpu.VMEM((4, LOCAL, 8 * 2 * HD), BF16),
            pltpu.VMEM((1, 32), jnp.int32),
            pltpu.VMEM((1, 32), jnp.int32),
            pltpu.VMEM((64, 128), jnp.int32),
            pltpu.VMEM((T, GROUP * HD), BF16),
            pltpu.VMEM((PARTS, VD, WIDTH), BF16),
            pltpu.VMEM((PARTS, LOCAL, WIDTH), F32),
            pltpu.VMEM((PARTS, TP, 8, 128), F32),
            pltpu.VMEM((PARTS, 3, 2, TOKENS, 2 * HD), BF16),
            pltpu.VMEM((PARTS, 3, 2, TOKENS, 2 * HD), BF16),
            pltpu.VMEM((PARTS, 2, TOKENS, 2 * HD), F32),
            pltpu.VMEM((PARTS, TOKENS, 2 * HD), BF16),
            pltpu.VMEM((PARTS, TOKENS, 2 * HD), BF16),
            pltpu.VMEM((WIDTH, WIDTH), BF16),
            pltpu.VMEM((2, T, 2 * HD), BF16),
            pltpu.VMEM((16, T, 2 * HD), BF16),
            pltpu.VMEM((PARTS, CTX, TOKENS, 2 * HD), BF16),
            pltpu.VMEM((2, 16, 128), jnp.int32),
            pltpu.VMEM((CTX, 128), jnp.int32),
            pltpu.VMEM((HD, GROUP * T), BF16),
            pltpu.VMEM((1, GROUP * T), F32),
            pltpu.VMEM((1, GROUP * T), F32),
            pltpu.VMEM((HD, GROUP * T), F32),
            dma(11), dma(PARTS), dma(PARTS), dma(3 * PARTS), dma(3 * PARTS), dma(3 * PARTS), dma(3 * PARTS),
            dma(7 * PARTS), dma(7 * PARTS), dma(3 * PARTS), dma(3 * PARTS), dma(PARTS), dma(PARTS),
            pltpu.SemaphoreType.REGULAR((2,)), dma(1), dma(1), dma(15), dma(16), pltpu.SemaphoreType.DMA((PARTS, 31)), pltpu.SemaphoreType.DMA((PARTS, CTX)),
        ],
        compiler_params=pltpu.CompilerParams(collective_id=0, has_side_effects=True, vmem_limit_bytes=60 * 2**20),
        name="window",
    )(
        jnp.transpose(vis_qkv, (1, 2, 0)),
        jnp.transpose(vis_resid),
        jnp.transpose(vis_out_w),
        merge_gain.reshape(1, LOCAL),
        merge_bias.reshape(1, LOCAL),
        vis_kv_w,
        frame_host.reshape(1, 32),
        vis_pos.reshape(1, 32),
        doc_ids.reshape(64, 128),
        text_kv.reshape(T, 2 * HD),
        queries,
    )


def solution(mesh):
    return jax.shard_map(
        shards,
        mesh=mesh,
        in_specs=(
            P(("dp", "ctx"), None, "tp"),
            P(("dp", "ctx"), "tp"),
            P(None, "tp"),
            P("tp"),
            P("tp"),
            P(None, "tp", None),
            P("dp"),
            P("dp"),
            P("dp"),
            P(("dp", "ctx"), "tp", None, None),
            P(("dp", "ctx"), "tp"),
        ),
        out_specs=P(("dp", "ctx"), "tp"),
        check_vma=False,
    )
```

```python
import functools
import math

import jax
import jax.numpy as jnp
from jax import lax
from jax.experimental import pallas as pl
from jax.experimental.pallas import tpu as pltpu
from jax.sharding import PartitionSpec as P

VD = 1280
VH = 16
HD = 128
FT = 128
FP = 512
T = 256
GROUP = 4
LOCAL = 160
HEAD = 80
CTX = 32
TP = 8
PARTS = 2
WIDTH = FP // PARTS
TOKENS = FT // PARTS
NEGATIVE = -1e30
LOG2E = math.log2(math.e)
MESH = pl.DeviceIdType.MESH
F32 = jnp.float32
BF16 = jnp.bfloat16


def dot_nt(a, b):
    return lax.dot_general(a, b, (((1,), (1,)), ((), ())), preferred_element_type=F32)


def dot_nn(a, b):
    return lax.dot_general(a, b, (((1,), (0,)), ((), ())), preferred_element_type=F32)


def eye(rows, cols, dtype):
    r = lax.broadcasted_iota(jnp.int32, (rows, cols), 0)
    c = lax.broadcasted_iota(jnp.int32, (rows, cols), 1)
    return jnp.where(r == c, 1.0, 0.0).astype(dtype)


class Spread:
    def __init__(self, buf, send, recv, place):
        self.buf, self.send, self.recv = buf, send, recv
        self.zl, self.y, self.tp, self.dp = place
        self.sent = []

    def copy(self, block, sem, zl, y):
        return pltpu.make_async_remote_copy(
            src_ref=self.buf.at[block],
            dst_ref=self.buf.at[block],
            send_sem=sem,
            recv_sem=self.recv.at[block],
            device_id=(zl * 4 + y, self.tp, self.dp),
            device_id_type=MESH,
        )

    def wait(self, block):
        self.copy(block, self.send.at[0], lax.rem(self.zl + 4, 8), self.y).wait_recv()

    def start(self, block, zl, y):
        copy = self.copy(block, self.send.at[len(self.sent)], zl, y)
        copy.start()
        self.sent.append(copy)

    def near(self, d):
        return (self.zl // 4) * 4 + lax.rem(self.zl + d, 4)

    def to_far(self, block):
        self.start(block, lax.rem(self.zl + 4, 8), self.y)

    def to_near(self, block):
        for d in (2, 3, 1):
            self.start(block, self.near(d), self.y)

    def to_y(self, block):
        for d in (2, 1, 3):
            self.start(block, self.zl, lax.rem(self.y + d, 4))

    def finish(self):
        for copy in self.sent:
            copy.wait_send()


def kernel(
    qkv_hbm, resid_hbm, out_w_hbm, gain_hbm, bias_hbm, kv_w_hbm, host_hbm, pos_hbm, docs_hbm, text, queries_hbm,
    out,
    qkv, resid, out_w, gain, bias, kv_w, host, pos, docs, queries, ctx, mine, stat, part_send, part_recv, part_own, pair_send, pair_recv, perm,
    raw, tbuf, vbuf, text_pos, frame_pos, qt, m_s, l_s, acc_s,
    load_sem, cz_s, cz_r, cx_s, cx_r, cf_s, cf_r, st_s, st_r, rx_s, rx_r, rz_s, rz_r,
    known, raw_s, raw_r, t_s, t_r, v_s, v_r,
):
    c = lax.axis_index("ctx")
    tp = lax.axis_index("tp")
    dp = lax.axis_index("dp")
    zl, y = c // 4, lax.rem(c, 4)
    zh, x = tp // 4, lax.rem(tp, 4)
    other = 1 - zh

    def at_tp(h, col):
        return (c, h * 4 + col, dp)

    def x_of(d):
        return lax.rem(x + d, 4)

    def along_z(d):
        z = lax.rem(zh * 8 + zl + d, 16)
        return (lax.rem(z, 8) * 4 + y, (z // 8) * 4 + x, dp)

    barrier = pltpu.get_barrier_semaphore()
    contacts = [along_z(4), along_z(12)]
    for d in (1, 2, 3):
        contacts.append(at_tp(zh, x_of(d)))
        contacts.append((zl * 4 + lax.rem(y + d, 4), tp, dp))
        contacts.append((((zl // 4) * 4 + lax.rem(zl + d, 4)) * 4 + y, tp, dp))
    for contact in contacts:
        pl.semaphore_signal(barrier, inc=1, device_id=contact, device_id_type=MESH)

    loads = []
    for source, target in (
        (qkv_hbm, qkv), (text, raw.at[zl // 4]), (pos_hbm, pos), (host_hbm, host), (docs_hbm, docs), (gain_hbm, gain),
        (bias_hbm, bias), (out_w_hbm, out_w), (resid_hbm, resid), (queries_hbm, queries), (kv_w_hbm, kv_w),
    ):
        loads.append(pltpu.make_async_copy(source, target, load_sem.at[len(loads)]))
        loads[-1].start()
    load_qkv, load_text, *load_rest, load_kv_w = loads

    place = (zl, y, tp, dp)
    texts = Spread(tbuf, t_s, t_r, place)
    frames = [Spread(vbuf.at[a], v_s.at[a], v_r.at[a], place) for a in range(PARTS)]
    pair = lax.rem(c, 16)
    quarter = lax.rem(zl, 4)
    load_qkv.wait()

    keys = dot_nt(eye(FP, FP, BF16), qkv[1]).astype(BF16)
    sent = []

    def ctx_copy(a, t, send, recv, target):
        rows = pl.ds(pl.multiple_of(t * LOCAL, 16), LOCAL)
        return pltpu.make_async_remote_copy(
            src_ref=ctx.at[a, rows],
            dst_ref=ctx.at[a, rows],
            send_sem=send,
            recv_sem=recv,
            device_id=target,
            device_id_type=MESH,
        )

    def begin(copy):
        copy.start()
        sent.append(copy)

    raw_copy = pltpu.make_async_remote_copy(
        src_ref=raw.at[zl // 4],
        dst_ref=raw.at[zl // 4],
        send_sem=raw_s.at[0],
        recv_sem=raw_r.at[0],
        device_id=(lax.rem(c + 16, CTX), tp, dp),
        device_id_type=MESH,
    )
    for h in range(2):
        head = slice(h * HEAD, (h + 1) * HEAD)
        scores = dot_nn(keys[:, head], qkv[0, head, :]) * (LOG2E / math.sqrt(HEAD))
        top = jnp.max(scores, axis=0, keepdims=True)
        weights = jnp.exp2(scores - top)
        total = jnp.sum(weights, axis=0, keepdims=True)
        mixed = (dot_nn(qkv[2, head, :], weights.astype(BF16)) / total).astype(BF16)
        for a in range(PARTS):
            ctx[a, pl.ds(pl.multiple_of(tp * LOCAL + h * HEAD, 16), HEAD), :] = mixed[:, a * WIDTH : (a + 1) * WIDTH]
        if h == 0:
            pl.semaphore_wait(barrier, len(contacts))
            for i, d in enumerate((4, 12)):
                pl.semaphore_signal(known.at[i], inc=1, device_id=along_z(d), device_id_type=MESH)
    load_text.wait()
    pl.semaphore_wait(known.at[0], 1)
    pl.semaphore_wait(known.at[1], 1)
    for a in range(PARTS):
        begin(ctx_copy(a, tp, cz_s.at[a], cz_r.at[a], at_tp(other, x)))
    for a in range(PARTS):
        for d in (2, 1, 3):
            begin(ctx_copy(a, tp, cx_s.at[a * 3 + d - 1], cx_r.at[a * 3 + d - 1], at_tp(zh, x_of(d))))

    for load in load_rest:
        load.wait()

    def slot_of(i):
        return FT * (2 * lax.broadcasted_iota(jnp.int32, (16, 32), 0) + (0, 1, 32, 33)[i])

    is_text = [jnp.max(jnp.where(slot_of(i) == pos[...], 1, 0), axis=1, keepdims=True) == 0 for i in range(4)]
    slots = [slot_of(i)[:, :1] for i in range(4)]
    early = jnp.where(is_text[0], slots[0], jnp.where(is_text[1], slots[1], slots[2]))
    late = jnp.where(is_text[3], slots[3], jnp.where(is_text[2], slots[2], slots[1]))
    text_pos[0] = jnp.broadcast_to(early, (16, 128))
    text_pos[1] = jnp.broadcast_to(late, (16, 128))
    owner = lax.broadcasted_iota(jnp.int32, (CTX, 32), 0)
    frame_col = jnp.sum(jnp.where(owner == host[...], pos[...], 0), axis=1, keepdims=True)
    frame_pos[...] = jnp.broadcast_to(frame_col, (CTX, 128))
    doc = jnp.concatenate([docs[pl.ds(2 * c, 1), :], docs[pl.ds(2 * c + 1, 1), :]], axis=1)
    first = jnp.zeros((1, T), jnp.int32)
    for d in (1, 2, 3):
        before = jnp.sum(jnp.where(docs[...] < d, 1, 0), axis=(0, 1), keepdims=True)
        first = jnp.where(doc == d, before, first)
    first = jnp.concatenate([first] * GROUP, axis=1)
    query_pos = c * T + lax.rem(lax.broadcasted_iota(jnp.int32, (1, GROUP * T), 1), T)
    m_s[...] = jnp.full(m_s.shape, NEGATIVE, F32)
    l_s[...] = jnp.zeros(l_s.shape, F32)
    acc_s[...] = jnp.zeros(acc_s.shape, F32)
    for g in range(GROUP):
        qt[:, g * T : (g + 1) * T] = dot_nt(eye(HD, HD, BF16), queries[:, g * HD : (g + 1) * HD]).astype(BF16)

    def attend(k, vt, starts):
        within = lax.broadcasted_iota(jnp.int32, (k.shape[0] // len(starts), GROUP * T), 0)
        key_pos = jnp.concatenate([within + jnp.concatenate([start] * 8, axis=1) for start in starts], axis=0)
        scores = dot_nn(k, qt[...]) * (LOG2E / math.sqrt(HD))
        scores = jnp.where((key_pos >= first) & (key_pos <= query_pos), scores, NEGATIVE)
        old = m_s[...]
        new = jnp.maximum(old, jnp.max(scores, axis=0, keepdims=True))
        weights = jnp.exp2(scores - new)
        factor = jnp.exp2(old - new)
        m_s[...] = new
        l_s[...] = l_s[...] * factor + jnp.sum(weights, axis=0, keepdims=True)
        acc_s[...] = acc_s[...] * factor + dot_nn(vt, weights.astype(BF16))

    def text_step(j, carry):
        layer = lax.rem(quarter + j, 4)
        for d in (1, 2, 3):
            texts.wait(layer * 4 + lax.rem(y + d, 4))

        @pl.when(layer <= zl)
        def _():
            held = [4 * layer + i for i in range(4)]
            blocks = [tbuf[h, i * FT : (i + 1) * FT] for h in held for i in range(2)]
            k = jnp.concatenate([b[:, :HD] for b in blocks], axis=0)
            vt = jnp.concatenate([b[:, HD:] for b in blocks], axis=1)
            attend(k, vt, [text_pos[i, pl.ds(h, 1), :] for h in held for i in range(2)])

        return carry

    def frame_step(a, j):
        layer = lax.rem(quarter + j, 4)
        for far in range(2):
            for d in (1, 2, 3):
                frames[a].wait((layer + 4 * far) * 4 + lax.rem(y + d, 4))

        @pl.when(layer <= zl)
        def _():
            held = [4 * layer + i + 16 * far for far in range(2) for i in range(4)]
            k = jnp.concatenate([vbuf[a, h, :, :HD] for h in held], axis=0)
            v = jnp.concatenate([vbuf[a, h, :, HD:] for h in held], axis=0)
            attend(k, v.T, [frame_pos[pl.ds(h, 1), :] + a * TOKENS for h in held])

    r = lax.broadcasted_iota(jnp.int32, (WIDTH, WIDTH), 0)
    p = lax.broadcasted_iota(jnp.int32, (WIDTH, WIDTH), 1)
    perm[...] = jnp.where((r % TOKENS) * 4 + r // TOKENS == p, 1.0, 0.0).astype(BF16)
    gain_col = jnp.sum(jnp.where(eye(LOCAL, LOCAL, F32) > 0, gain[...], 0.0), axis=1, keepdims=True)
    bias_col = jnp.sum(jnp.where(eye(LOCAL, LOCAL, F32) > 0, bias[...], 0.0), axis=1, keepdims=True)

    def compact():
        raw_copy.wait_recv()
        four = [raw[i, j * FT : (j + 1) * FT].astype(F32) for i in range(2) for j in range(2)]
        for which in range(2):
            start = text_pos[which, pl.ds(pair, 1), :]
            start = start.reshape(1, 1, HD)
            chosen = four[3]
            for i in range(3):
                chosen = jnp.where(start == FT * (2 * pair + (0, 1, 32)[i]), four[i], chosen)
            tbuf[pair, which * FT : (which + 1) * FT, :HD] = chosen[:, 0, :].astype(BF16)
            tbuf[pair, which * FT : (which + 1) * FT, HD:] = chosen[:, 1, :].T.astype(BF16)
        texts.to_near(pair)
        texts.to_y(pair)

    for a in range(PARTS):
        ctx_copy(a, other * 4 + x, cz_s.at[a], cz_r.at[a], at_tp(other, x)).wait_recv()
        for d in (2, 1, 3):
            begin(ctx_copy(a, other * 4 + x, cf_s.at[a * 3 + d - 1], cf_r.at[a * 3 + d - 1], at_tp(zh, x_of(d))))
        if a == 0:
            begin(raw_copy)
    half = lambda i: pl.ds(pl.multiple_of(i * (VD // 2), 128), VD // 2)

    def stat_copy(a, t, d, target):
        return pltpu.make_async_remote_copy(
            src_ref=stat.at[a, t],
            dst_ref=stat.at[a, t],
            send_sem=st_s.at[a * 7 + d - 1],
            recv_sem=st_r.at[a * 7 + d - 1],
            device_id=(c, target, dp),
            device_id_type=MESH,
        )

    lanes = WIDTH // 128
    for a in range(PARTS):
        for d in (1, 2, 3):
            ctx_copy(a, zh * 4 + x_of(4 - d), cx_s.at[0], cx_r.at[a * 3 + d - 1], at_tp(zh, x_of(d))).wait_recv()
        hidden = resid[:, a * WIDTH : (a + 1) * WIDTH].astype(F32) + dot_nn(out_w[:, half(zh)], ctx[a, half(zh), :])
        for d in (1, 2, 3):
            ctx_copy(a, other * 4 + x_of(4 - d), cf_s.at[0], cf_r.at[a * 3 + d - 1], at_tp(zh, x_of(d))).wait_recv()
        hidden = hidden + dot_nn(out_w[:, half(other)], ctx[a, half(other), :])
        mine[a] = hidden
        sums = jnp.sum(hidden, axis=0, keepdims=True)
        squares = jnp.sum(hidden * hidden, axis=0, keepdims=True)
        stat[a, tp] = jnp.zeros((8, 128), F32)
        for i in range(lanes):
            stat[a, tp, i : i + 1, :] = sums[:, i * 128 : (i + 1) * 128]
            stat[a, tp, 4 + i : 5 + i, :] = squares[:, i * 128 : (i + 1) * 128]
        for d in (6, 2, 4, 5, 3, 1, 7):
            begin(stat_copy(a, tp, d, lax.rem(tp + d, TP)))

    load_kv_w.wait()

    def part_copy(a, d):
        return pltpu.make_async_remote_copy(
            src_ref=part_send.at[a, d - 1],
            dst_ref=part_recv.at[a, d - 1],
            send_sem=rx_s.at[a * 3 + d - 1],
            recv_sem=rx_r.at[a * 3 + d - 1],
            device_id=at_tp(zh, x_of(d)),
            device_id_type=MESH,
        )

    for a in range(PARTS):
        for d in range(1, TP):
            stat_copy(a, lax.rem(tp + TP - d, TP), d, lax.rem(tp + d, TP)).wait_recv()
        all_stats = stat[a, 0]
        for t in range(1, TP):
            all_stats = all_stats + stat[a, t]
        mean = all_stats[0:4] * (1.0 / VD)
        scale = lax.rsqrt(all_stats[4:8] * (1.0 / VD) - mean * mean + 1e-6)
        mean_row = jnp.concatenate([mean[i : i + 1] for i in range(lanes)], axis=1)
        scale_row = jnp.concatenate([scale[i : i + 1] for i in range(lanes)], axis=1)
        normed = ((mine[a] - mean_row) * scale_row * gain_col + bias_col).astype(BF16)
        grouped = dot_nt(perm[...], normed).astype(BF16)

        def partial_kv(t):
            cols = pl.ds(pl.multiple_of(t * 2 * HD, 128), 2 * HD)
            total = dot_nn(grouped[:TOKENS], kv_w[0, :, cols])
            for j in range(1, 4):
                total = total + dot_nn(grouped[j * TOKENS : (j + 1) * TOKENS], kv_w[j, :, cols])
            return total

        for d in (2, 1, 3):
            for i in range(2):
                part_send[a, d - 1, i] = partial_kv(i * 4 + x_of(d)).astype(BF16)
            begin(part_copy(a, d))
        if a == 0:
            compact()
        part_own[a, 0] = partial_kv(other * 4 + x)
        part_own[a, 1] = partial_kv(zh * 4 + x)

    def summed(a, slot, which):
        total = part_own[a, slot]
        for d in range(3):
            total = total + part_recv[a, d, which].astype(F32)
        return total

    def pair_copy(a):
        return pltpu.make_async_remote_copy(
            src_ref=pair_send.at[a],
            dst_ref=pair_recv.at[a],
            send_sem=rz_s.at[a],
            recv_sem=rz_r.at[a],
            device_id=at_tp(other, x),
            device_id_type=MESH,
        )

    for a in range(PARTS):
        for d in (1, 2, 3):
            part_copy(a, d).wait_recv()
        pair_send[a] = summed(a, 0, other).astype(BF16)
        begin(pair_copy(a))
        part_own[a, 1] = summed(a, 1, zh)
    for d in (2, 1, 3):
        block = lax.rem(quarter + d, 4) * 4 + y
        texts.wait(block)
        texts.to_y(block)
    text_step(0, 0)
    far = lax.rem(c + 16, CTX)
    for a in range(PARTS):
        pair_copy(a).wait_recv()
        vbuf[a, c] = (part_own[a, 1] + pair_recv[a].astype(F32)).astype(BF16)
        frames[a].to_far(c)
        frames[a].to_near(c)
        frames[a].to_y(c)
    for a in range(PARTS):
        frames[a].wait(far)
        frames[a].to_near(far)
        frames[a].to_y(far)
        for d in (2, 1, 3):
            block = frames[a].near(d) * 4 + y
            frames[a].wait(block)
            frames[a].to_y(block)
    lax.fori_loop(1, 3, text_step, 0)
    for a in range(PARTS):
        for d in (2, 1, 3):
            block = lax.rem(frames[a].near(d) + 4, 8) * 4 + y
            frames[a].wait(block)
            frames[a].to_y(block)
    lax.fori_loop(3, 4, text_step, 0)
    for a in range(PARTS):

        def step(j, carry):
            frame_step(a, j)
            return carry

        lax.fori_loop(0, 4, step, 0)

    for g in range(GROUP):
        cols = slice(g * T, (g + 1) * T)
        result = (acc_s[:, cols] / l_s[:, cols]).astype(BF16)
        out[:, g * HD : (g + 1) * HD] = dot_nt(eye(T, T, BF16), result).astype(BF16)
    for copy in sent:
        copy.wait_send()
    texts.finish()
    for part in frames:
        part.finish()


def shards(
    vis_qkv, vis_resid, vis_out_w, merge_gain, merge_bias, vis_kv_w, frame_host, vis_pos, doc_ids, text_kv, queries
):
    vmem = pl.BlockSpec(memory_space=pltpu.VMEM)
    hbm = pl.BlockSpec(memory_space=pl.ANY)
    dma = lambda n: pltpu.SemaphoreType.DMA((n,))
    return pl.pallas_call(
        kernel,
        out_shape=jax.ShapeDtypeStruct((T, GROUP * HD), BF16),
        in_specs=[hbm] * 11,
        out_specs=vmem,
        scratch_shapes=[
            pltpu.VMEM((3, LOCAL, FP), BF16),
            pltpu.VMEM((LOCAL, FP), BF16),
            pltpu.VMEM((LOCAL, VD), BF16),
            pltpu.VMEM((1, LOCAL), F32),
            pltpu.VMEM((1, LOCAL), F32),
            pltpu.VMEM((4, LOCAL, 8 * 2 * HD), BF16),
            pltpu.VMEM((1, 32), jnp.int32),
            pltpu.VMEM((1, 32), jnp.int32),
            pltpu.VMEM((64, 128), jnp.int32),
            pltpu.VMEM((T, GROUP * HD), BF16),
            pltpu.VMEM((PARTS, VD, WIDTH), BF16),
            pltpu.VMEM((PARTS, LOCAL, WIDTH), F32),
            pltpu.VMEM((PARTS, TP, 8, 128), F32),
            pltpu.VMEM((PARTS, 3, 2, TOKENS, 2 * HD), BF16),
            pltpu.VMEM((PARTS, 3, 2, TOKENS, 2 * HD), BF16),
            pltpu.VMEM((PARTS, 2, TOKENS, 2 * HD), F32),
            pltpu.VMEM((PARTS, TOKENS, 2 * HD), BF16),
            pltpu.VMEM((PARTS, TOKENS, 2 * HD), BF16),
            pltpu.VMEM((WIDTH, WIDTH), BF16),
            pltpu.VMEM((2, T, 2, HD), BF16),
            pltpu.VMEM((16, T, 2 * HD), BF16),
            pltpu.VMEM((PARTS, CTX, TOKENS, 2 * HD), BF16),
            pltpu.VMEM((2, 16, 128), jnp.int32),
            pltpu.VMEM((CTX, 128), jnp.int32),
            pltpu.VMEM((HD, GROUP * T), BF16),
            pltpu.VMEM((1, GROUP * T), F32),
            pltpu.VMEM((1, GROUP * T), F32),
            pltpu.VMEM((HD, GROUP * T), F32),
            dma(11), dma(PARTS), dma(PARTS), dma(3 * PARTS), dma(3 * PARTS), dma(3 * PARTS), dma(3 * PARTS),
            dma(7 * PARTS), dma(7 * PARTS), dma(3 * PARTS), dma(3 * PARTS), dma(PARTS), dma(PARTS),
            pltpu.SemaphoreType.REGULAR((2,)), dma(1), dma(1), dma(15), dma(16), pltpu.SemaphoreType.DMA((PARTS, 31)), pltpu.SemaphoreType.DMA((PARTS, CTX)),
        ],
        compiler_params=pltpu.CompilerParams(collective_id=0, has_side_effects=True, vmem_limit_bytes=60 * 2**20),
        name="window",
    )(
        jnp.transpose(vis_qkv, (1, 2, 0)),
        jnp.transpose(vis_resid),
        jnp.transpose(vis_out_w),
        merge_gain.reshape(1, LOCAL),
        merge_bias.reshape(1, LOCAL),
        vis_kv_w,
        frame_host.reshape(1, 32),
        vis_pos.reshape(1, 32),
        doc_ids.reshape(64, 128),
        text_kv.reshape(T, 2, HD),
        queries,
    )


def solution(mesh):
    return jax.shard_map(
        shards,
        mesh=mesh,
        in_specs=(
            P(("dp", "ctx"), None, "tp"),
            P(("dp", "ctx"), "tp"),
            P(None, "tp"),
            P("tp"),
            P("tp"),
            P(None, "tp", None),
            P("dp"),
            P("dp"),
            P("dp"),
            P(("dp", "ctx"), "tp", None, None),
            P(("dp", "ctx"), "tp"),
        ),
        out_specs=P(("dp", "ctx"), "tp"),
        check_vma=False,
    )
```

```python
import functools
import math

import jax
import jax.numpy as jnp
from jax import lax
from jax.experimental import pallas as pl
from jax.experimental.pallas import tpu as pltpu
from jax.sharding import PartitionSpec as P

VD = 1280
VH = 16
HD = 128
FT = 128
FP = 512
T = 256
GROUP = 4
LOCAL = 160
HEAD = 80
CTX = 32
TP = 8
PARTS = 2
WIDTH = FP // PARTS
TOKENS = FT // PARTS
NEGATIVE = -1e30
LOG2E = math.log2(math.e)
MESH = pl.DeviceIdType.MESH
F32 = jnp.float32
BF16 = jnp.bfloat16


def dot_nt(a, b):
    return lax.dot_general(a, b, (((1,), (1,)), ((), ())), preferred_element_type=F32)


def dot_nn(a, b):
    return lax.dot_general(a, b, (((1,), (0,)), ((), ())), preferred_element_type=F32)


def eye(rows, cols, dtype):
    r = lax.broadcasted_iota(jnp.int32, (rows, cols), 0)
    c = lax.broadcasted_iota(jnp.int32, (rows, cols), 1)
    return jnp.where(r == c, 1.0, 0.0).astype(dtype)


class Spread:
    def __init__(self, buf, send, recv, place):
        self.buf, self.send, self.recv = buf, send, recv
        self.zl, self.y, self.tp, self.dp = place
        self.sent = []

    def copy(self, block, sem, zl, y):
        return pltpu.make_async_remote_copy(
            src_ref=self.buf.at[block],
            dst_ref=self.buf.at[block],
            send_sem=sem,
            recv_sem=self.recv.at[block],
            device_id=(zl * 4 + y, self.tp, self.dp),
            device_id_type=MESH,
        )

    def wait(self, block):
        self.copy(block, self.send.at[0], lax.rem(self.zl + 4, 8), self.y).wait_recv()

    def start(self, block, zl, y):
        copy = self.copy(block, self.send.at[len(self.sent)], zl, y)
        copy.start()
        self.sent.append(copy)

    def near(self, d):
        return (self.zl // 4) * 4 + lax.rem(self.zl + d, 4)

    def to_far(self, block):
        self.start(block, lax.rem(self.zl + 4, 8), self.y)

    def to_near(self, block):
        for d in (2, 3, 1):
            self.start(block, self.near(d), self.y)

    def to_y(self, block):
        for d in (2, 1, 3):
            self.start(block, self.zl, lax.rem(self.y + d, 4))

    def finish(self):
        for copy in self.sent:
            copy.wait_send()


def kernel(
    qkv_hbm, resid_hbm, out_w_hbm, gain_hbm, bias_hbm, kv_w_hbm, host_hbm, pos_hbm, docs_hbm, text, queries_hbm,
    out,
    qkv, resid, out_w, gain, bias, kv_w, host, pos, docs, queries, ctx, mine, stat, part_send, part_recv, part_own, pair_send, pair_recv, perm,
    raw, tbuf, vbuf, text_pos, frame_pos, qt, m_s, l_s, acc_s,
    load_sem, cz_s, cz_r, cx_s, cx_r, cf_s, cf_r, st_s, st_r, rx_s, rx_r, rz_s, rz_r,
    known, raw_s, raw_r, t_s, t_r, v_s, v_r,
):
    c = lax.axis_index("ctx")
    tp = lax.axis_index("tp")
    dp = lax.axis_index("dp")
    zl, y = c // 4, lax.rem(c, 4)
    zh, x = tp // 4, lax.rem(tp, 4)
    other = 1 - zh

    def at_tp(h, col):
        return (c, h * 4 + col, dp)

    def x_of(d):
        return lax.rem(x + d, 4)

    def along_z(d):
        z = lax.rem(zh * 8 + zl + d, 16)
        return (lax.rem(z, 8) * 4 + y, (z // 8) * 4 + x, dp)

    barrier = pltpu.get_barrier_semaphore()
    contacts = [along_z(4), along_z(12)]
    for d in (1, 2, 3):
        contacts.append(at_tp(zh, x_of(d)))
        contacts.append((zl * 4 + lax.rem(y + d, 4), tp, dp))
        contacts.append((((zl // 4) * 4 + lax.rem(zl + d, 4)) * 4 + y, tp, dp))
    for contact in contacts:
        pl.semaphore_signal(barrier, inc=1, device_id=contact, device_id_type=MESH)

    loads = []
    for source, target in (
        (qkv_hbm, qkv), (text, raw.at[zl // 4]), (pos_hbm, pos), (host_hbm, host), (docs_hbm, docs), (gain_hbm, gain),
        (bias_hbm, bias), (out_w_hbm, out_w), (resid_hbm, resid), (queries_hbm, queries), (kv_w_hbm, kv_w),
    ):
        loads.append(pltpu.make_async_copy(source, target, load_sem.at[len(loads)]))
        loads[-1].start()
    load_qkv, load_text, *load_rest, load_kv_w = loads

    place = (zl, y, tp, dp)
    texts = Spread(tbuf, t_s, t_r, place)
    frames = [Spread(vbuf.at[a], v_s.at[a], v_r.at[a], place) for a in range(PARTS)]
    pair = lax.rem(c, 16)
    quarter = lax.rem(zl, 4)
    load_qkv.wait()

    keys = dot_nt(eye(FP, FP, BF16), qkv[1]).astype(BF16)
    sent = []

    def ctx_copy(a, t, send, recv, target):
        rows = pl.ds(pl.multiple_of(t * LOCAL, 16), LOCAL)
        return pltpu.make_async_remote_copy(
            src_ref=ctx.at[a, rows],
            dst_ref=ctx.at[a, rows],
            send_sem=send,
            recv_sem=recv,
            device_id=target,
            device_id_type=MESH,
        )

    def begin(copy):
        copy.start()
        sent.append(copy)

    raw_copy = pltpu.make_async_remote_copy(
        src_ref=raw.at[zl // 4],
        dst_ref=raw.at[zl // 4],
        send_sem=raw_s.at[0],
        recv_sem=raw_r.at[0],
        device_id=(lax.rem(c + 16, CTX), tp, dp),
        device_id_type=MESH,
    )
    for h in range(2):
        head = slice(h * HEAD, (h + 1) * HEAD)
        scores = dot_nn(keys[:, head], qkv[0, head, :]) * (LOG2E / math.sqrt(HEAD))
        top = jnp.max(scores, axis=0, keepdims=True)
        weights = jnp.exp2(scores - top)
        total = jnp.sum(weights, axis=0, keepdims=True)
        mixed = (dot_nn(qkv[2, head, :], weights.astype(BF16)) / total).astype(BF16)
        for a in range(PARTS):
            ctx[a, pl.ds(pl.multiple_of(tp * LOCAL + h * HEAD, 16), HEAD), :] = mixed[:, a * WIDTH : (a + 1) * WIDTH]
        if h == 0:
            pl.semaphore_wait(barrier, len(contacts))
            for i, d in enumerate((4, 12)):
                pl.semaphore_signal(known.at[i], inc=1, device_id=along_z(d), device_id_type=MESH)
    load_text.wait()
    pl.semaphore_wait(known.at[0], 1)
    pl.semaphore_wait(known.at[1], 1)
    for a in range(PARTS):
        begin(ctx_copy(a, tp, cz_s.at[a], cz_r.at[a], at_tp(other, x)))
    for a in range(PARTS):
        for d in (2, 1, 3):
            begin(ctx_copy(a, tp, cx_s.at[a * 3 + d - 1], cx_r.at[a * 3 + d - 1], at_tp(zh, x_of(d))))

    for load in load_rest:
        load.wait()

    def slot_of(i):
        return FT * (2 * lax.broadcasted_iota(jnp.int32, (16, 32), 0) + (0, 1, 32, 33)[i])

    is_text = [jnp.max(jnp.where(slot_of(i) == pos[...], 1, 0), axis=1, keepdims=True) == 0 for i in range(4)]
    slots = [slot_of(i)[:, :1] for i in range(4)]
    early = jnp.where(is_text[0], slots[0], jnp.where(is_text[1], slots[1], slots[2]))
    late = jnp.where(is_text[3], slots[3], jnp.where(is_text[2], slots[2], slots[1]))
    text_pos[0] = jnp.broadcast_to(early, (16, 128))
    text_pos[1] = jnp.broadcast_to(late, (16, 128))
    owner = lax.broadcasted_iota(jnp.int32, (CTX, 32), 0)
    frame_col = jnp.sum(jnp.where(owner == host[...], pos[...], 0), axis=1, keepdims=True)
    frame_pos[...] = jnp.broadcast_to(frame_col, (CTX, 128))
    doc = jnp.concatenate([docs[pl.ds(2 * c, 1), :], docs[pl.ds(2 * c + 1, 1), :]], axis=1)
    first = jnp.zeros((1, T), jnp.int32)
    for d in (1, 2, 3):
        before = jnp.sum(jnp.where(docs[...] < d, 1, 0), axis=(0, 1), keepdims=True)
        first = jnp.where(doc == d, before, first)
    first = jnp.concatenate([first] * GROUP, axis=1)
    query_pos = c * T + lax.rem(lax.broadcasted_iota(jnp.int32, (1, GROUP * T), 1), T)
    m_s[...] = jnp.full(m_s.shape, NEGATIVE, F32)
    l_s[...] = jnp.zeros(l_s.shape, F32)
    acc_s[...] = jnp.zeros(acc_s.shape, F32)
    for g in range(GROUP):
        qt[:, g * T : (g + 1) * T] = dot_nt(eye(HD, HD, BF16), queries[:, g * HD : (g + 1) * HD]).astype(BF16)

    def attend(k, vt, starts):
        within = lax.broadcasted_iota(jnp.int32, (k.shape[0] // len(starts), GROUP * T), 0)
        key_pos = jnp.concatenate([within + jnp.concatenate([start] * 8, axis=1) for start in starts], axis=0)
        scores = dot_nn(k, qt[...]) * (LOG2E / math.sqrt(HD))
        scores = jnp.where((key_pos >= first) & (key_pos <= query_pos), scores, NEGATIVE)
        old = m_s[...]
        new = jnp.maximum(old, jnp.max(scores, axis=0, keepdims=True))
        weights = jnp.exp2(scores - new)
        factor = jnp.exp2(old - new)
        m_s[...] = new
        l_s[...] = l_s[...] * factor + jnp.sum(weights, axis=0, keepdims=True)
        acc_s[...] = acc_s[...] * factor + dot_nn(vt, weights.astype(BF16))

    def text_step(j, carry):
        layer = lax.rem(quarter + j, 4)
        for d in (1, 2, 3):
            texts.wait(layer * 4 + lax.rem(y + d, 4))

        @pl.when(layer <= zl)
        def _():
            held = [4 * layer + i for i in range(4)]
            blocks = [tbuf[h, i * FT : (i + 1) * FT] for h in held for i in range(2)]
            k = jnp.concatenate([b[:, :HD] for b in blocks], axis=0)
            vt = jnp.concatenate([b[:, HD:] for b in blocks], axis=1)
            attend(k, vt, [text_pos[i, pl.ds(h, 1), :] for h in held for i in range(2)])

        return carry

    def frame_step(a, j):
        layer = lax.rem(quarter + j, 4)
        for far in range(2):
            for d in (1, 2, 3):
                frames[a].wait((layer + 4 * far) * 4 + lax.rem(y + d, 4))

        @pl.when(layer <= zl)
        def _():
            held = [4 * layer + i + 16 * far for far in range(2) for i in range(4)]
            k = jnp.concatenate([vbuf[a, h, :, :HD] for h in held], axis=0)
            v = jnp.concatenate([vbuf[a, h, :, HD:] for h in held], axis=0)
            attend(k, v.T, [frame_pos[pl.ds(h, 1), :] + a * TOKENS for h in held])

    r = lax.broadcasted_iota(jnp.int32, (WIDTH, WIDTH), 0)
    p = lax.broadcasted_iota(jnp.int32, (WIDTH, WIDTH), 1)
    perm[...] = jnp.where((r % TOKENS) * 4 + r // TOKENS == p, 1.0, 0.0).astype(BF16)
    gain_col = jnp.sum(jnp.where(eye(LOCAL, LOCAL, F32) > 0, gain[...], 0.0), axis=1, keepdims=True)
    bias_col = jnp.sum(jnp.where(eye(LOCAL, LOCAL, F32) > 0, bias[...], 0.0), axis=1, keepdims=True)

    def compact():
        raw_copy.wait_recv()
        four = [raw[i, j * FT : (j + 1) * FT].astype(F32) for i in range(2) for j in range(2)]
        for which in range(2):
            start = text_pos[which, pl.ds(pair, 1), :]
            start = start.reshape(1, 1, HD)
            chosen = four[3]
            for i in range(3):
                chosen = jnp.where(start == FT * (2 * pair + (0, 1, 32)[i]), four[i], chosen)
            tbuf[pair, which * FT : (which + 1) * FT, :HD] = chosen[:, 0, :].astype(BF16)
            tbuf[pair, which * FT : (which + 1) * FT, HD:] = chosen[:, 1, :].T.astype(BF16)
        texts.to_near(pair)
        texts.to_y(pair)

    for a in range(PARTS):
        ctx_copy(a, other * 4 + x, cz_s.at[a], cz_r.at[a], at_tp(other, x)).wait_recv()
        for d in (2, 1, 3):
            begin(ctx_copy(a, other * 4 + x, cf_s.at[a * 3 + d - 1], cf_r.at[a * 3 + d - 1], at_tp(zh, x_of(d))))
        if a == 0:
            begin(raw_copy)
    half = lambda i: pl.ds(pl.multiple_of(i * (VD // 2), 128), VD // 2)

    def stat_copy(a, t, d, target):
        return pltpu.make_async_remote_copy(
            src_ref=stat.at[a, t],
            dst_ref=stat.at[a, t],
            send_sem=st_s.at[a * 7 + d - 1],
            recv_sem=st_r.at[a * 7 + d - 1],
            device_id=(c, target, dp),
            device_id_type=MESH,
        )

    lanes = WIDTH // 128
    for a in range(PARTS):
        for d in (1, 2, 3):
            ctx_copy(a, zh * 4 + x_of(4 - d), cx_s.at[0], cx_r.at[a * 3 + d - 1], at_tp(zh, x_of(d))).wait_recv()
        hidden = resid[:, a * WIDTH : (a + 1) * WIDTH].astype(F32) + dot_nn(out_w[:, half(zh)], ctx[a, half(zh), :])
        for d in (1, 2, 3):
            ctx_copy(a, other * 4 + x_of(4 - d), cf_s.at[0], cf_r.at[a * 3 + d - 1], at_tp(zh, x_of(d))).wait_recv()
        hidden = hidden + dot_nn(out_w[:, half(other)], ctx[a, half(other), :])
        mine[a] = hidden
        sums = jnp.sum(hidden, axis=0, keepdims=True)
        squares = jnp.sum(hidden * hidden, axis=0, keepdims=True)
        stat[a, tp] = jnp.zeros((8, 128), F32)
        for i in range(lanes):
            stat[a, tp, i : i + 1, :] = sums[:, i * 128 : (i + 1) * 128]
            stat[a, tp, 4 + i : 5 + i, :] = squares[:, i * 128 : (i + 1) * 128]
        for d in (6, 2, 4, 5, 3, 1, 7):
            begin(stat_copy(a, tp, d, lax.rem(tp + d, TP)))

    load_kv_w.wait()

    def part_copy(a, d):
        return pltpu.make_async_remote_copy(
            src_ref=part_send.at[a, d - 1],
            dst_ref=part_recv.at[a, d - 1],
            send_sem=rx_s.at[a * 3 + d - 1],
            recv_sem=rx_r.at[a * 3 + d - 1],
            device_id=at_tp(zh, x_of(d)),
            device_id_type=MESH,
        )

    for a in range(PARTS):
        for d in range(1, TP):
            stat_copy(a, lax.rem(tp + TP - d, TP), d, lax.rem(tp + d, TP)).wait_recv()
        all_stats = stat[a, 0]
        for t in range(1, TP):
            all_stats = all_stats + stat[a, t]
        mean = all_stats[0:4] * (1.0 / VD)
        scale = lax.rsqrt(all_stats[4:8] * (1.0 / VD) - mean * mean + 1e-6)
        mean_row = jnp.concatenate([mean[i : i + 1] for i in range(lanes)], axis=1)
        scale_row = jnp.concatenate([scale[i : i + 1] for i in range(lanes)], axis=1)
        normed = ((mine[a] - mean_row) * scale_row * gain_col + bias_col).astype(BF16)
        grouped = dot_nt(perm[...], normed).astype(BF16)

        def partial_kv(t):
            cols = pl.ds(pl.multiple_of(t * 2 * HD, 128), 2 * HD)
            total = dot_nn(grouped[:TOKENS], kv_w[0, :, cols])
            for j in range(1, 4):
                total = total + dot_nn(grouped[j * TOKENS : (j + 1) * TOKENS], kv_w[j, :, cols])
            return total

        for d in (2, 1, 3):
            for i in range(2):
                part_send[a, d - 1, i] = partial_kv(i * 4 + x_of(d)).astype(BF16)
            begin(part_copy(a, d))
        if a == 0:
            compact()
        part_own[a, 0] = partial_kv(other * 4 + x)
        part_own[a, 1] = partial_kv(zh * 4 + x)

    def summed(a, slot, which):
        total = part_own[a, slot]
        for d in range(3):
            total = total + part_recv[a, d, which].astype(F32)
        return total

    def pair_copy(a):
        return pltpu.make_async_remote_copy(
            src_ref=pair_send.at[a],
            dst_ref=pair_recv.at[a],
            send_sem=rz_s.at[a],
            recv_sem=rz_r.at[a],
            device_id=at_tp(other, x),
            device_id_type=MESH,
        )

    for a in range(PARTS):
        for d in (1, 2, 3):
            part_copy(a, d).wait_recv()
        pair_send[a] = summed(a, 0, other).astype(BF16)
        begin(pair_copy(a))
        part_own[a, 1] = summed(a, 1, zh)
    for d in (2, 1, 3):
        block = lax.rem(quarter + d, 4) * 4 + y
        texts.wait(block)
        texts.to_y(block)
    text_step(0, 0)
    far = lax.rem(c + 16, CTX)
    for a in range(PARTS):
        pair_copy(a).wait_recv()
        vbuf[a, c] = (part_own[a, 1] + pair_recv[a].astype(F32)).astype(BF16)
        frames[a].to_far(c)
        frames[a].to_near(c)
        frames[a].to_y(c)
    for a in range(PARTS):
        frames[a].wait(far)
        frames[a].to_near(far)
        frames[a].to_y(far)
    for a in range(PARTS):
        for d in (2, 1, 3):
            block = frames[a].near(d) * 4 + y
            frames[a].wait(block)
            frames[a].to_y(block)
    lax.fori_loop(1, 3, text_step, 0)
    for a in range(PARTS):
        for d in (2, 1, 3):
            block = lax.rem(frames[a].near(d) + 4, 8) * 4 + y
            frames[a].wait(block)
            frames[a].to_y(block)
    lax.fori_loop(3, 4, text_step, 0)
    for a in range(PARTS):

        def step(j, carry):
            frame_step(a, j)
            return carry

        lax.fori_loop(0, 4, step, 0)

    for g in range(GROUP):
        cols = slice(g * T, (g + 1) * T)
        result = (acc_s[:, cols] / l_s[:, cols]).astype(BF16)
        out[:, g * HD : (g + 1) * HD] = dot_nt(eye(T, T, BF16), result).astype(BF16)
    for copy in sent:
        copy.wait_send()
    texts.finish()
    for part in frames:
        part.finish()


def shards(
    vis_qkv, vis_resid, vis_out_w, merge_gain, merge_bias, vis_kv_w, frame_host, vis_pos, doc_ids, text_kv, queries
):
    vmem = pl.BlockSpec(memory_space=pltpu.VMEM)
    hbm = pl.BlockSpec(memory_space=pl.ANY)
    dma = lambda n: pltpu.SemaphoreType.DMA((n,))
    return pl.pallas_call(
        kernel,
        out_shape=jax.ShapeDtypeStruct((T, GROUP * HD), BF16),
        in_specs=[hbm] * 11,
        out_specs=vmem,
        scratch_shapes=[
            pltpu.VMEM((3, LOCAL, FP), BF16),
            pltpu.VMEM((LOCAL, FP), BF16),
            pltpu.VMEM((LOCAL, VD), BF16),
            pltpu.VMEM((1, LOCAL), F32),
            pltpu.VMEM((1, LOCAL), F32),
            pltpu.VMEM((4, LOCAL, 8 * 2 * HD), BF16),
            pltpu.VMEM((1, 32), jnp.int32),
            pltpu.VMEM((1, 32), jnp.int32),
            pltpu.VMEM((64, 128), jnp.int32),
            pltpu.VMEM((T, GROUP * HD), BF16),
            pltpu.VMEM((PARTS, VD, WIDTH), BF16),
            pltpu.VMEM((PARTS, LOCAL, WIDTH), F32),
            pltpu.VMEM((PARTS, TP, 8, 128), F32),
            pltpu.VMEM((PARTS, 3, 2, TOKENS, 2 * HD), BF16),
            pltpu.VMEM((PARTS, 3, 2, TOKENS, 2 * HD), BF16),
            pltpu.VMEM((PARTS, 2, TOKENS, 2 * HD), F32),
            pltpu.VMEM((PARTS, TOKENS, 2 * HD), BF16),
            pltpu.VMEM((PARTS, TOKENS, 2 * HD), BF16),
            pltpu.VMEM((WIDTH, WIDTH), BF16),
            pltpu.VMEM((2, T, 2, HD), BF16),
            pltpu.VMEM((16, T, 2 * HD), BF16),
            pltpu.VMEM((PARTS, CTX, TOKENS, 2 * HD), BF16),
            pltpu.VMEM((2, 16, 128), jnp.int32),
            pltpu.VMEM((CTX, 128), jnp.int32),
            pltpu.VMEM((HD, GROUP * T), BF16),
            pltpu.VMEM((1, GROUP * T), F32),
            pltpu.VMEM((1, GROUP * T), F32),
            pltpu.VMEM((HD, GROUP * T), F32),
            dma(11), dma(PARTS), dma(PARTS), dma(3 * PARTS), dma(3 * PARTS), dma(3 * PARTS), dma(3 * PARTS),
            dma(7 * PARTS), dma(7 * PARTS), dma(3 * PARTS), dma(3 * PARTS), dma(PARTS), dma(PARTS),
            pltpu.SemaphoreType.REGULAR((2,)), dma(1), dma(1), dma(15), dma(16), pltpu.SemaphoreType.DMA((PARTS, 31)), pltpu.SemaphoreType.DMA((PARTS, CTX)),
        ],
        compiler_params=pltpu.CompilerParams(collective_id=0, has_side_effects=True, vmem_limit_bytes=60 * 2**20),
        name="window",
    )(
        jnp.transpose(vis_qkv, (1, 2, 0)),
        jnp.transpose(vis_resid),
        jnp.transpose(vis_out_w),
        merge_gain.reshape(1, LOCAL),
        merge_bias.reshape(1, LOCAL),
        vis_kv_w,
        frame_host.reshape(1, 32),
        vis_pos.reshape(1, 32),
        doc_ids.reshape(64, 128),
        text_kv.reshape(T, 2, HD),
        queries,
    )


def solution(mesh):
    return jax.shard_map(
        shards,
        mesh=mesh,
        in_specs=(
            P(("dp", "ctx"), None, "tp"),
            P(("dp", "ctx"), "tp"),
            P(None, "tp"),
            P("tp"),
            P("tp"),
            P(None, "tp", None),
            P("dp"),
            P("dp"),
            P("dp"),
            P(("dp", "ctx"), "tp", None, None),
            P(("dp", "ctx"), "tp"),
        ),
        out_specs=P(("dp", "ctx"), "tp"),
        check_vma=False,
    )
```
